32 devices in a mesh: grp: 2 (over x), row: 16 (over z, y, core).
Axes of the slice: x: 2, y: 2, z: 4, core: 2. Of those that a mesh axis runs over, the one named last changes fastest.
Arguments:
- tokens: bfloat16 [4096, 3072], P(('grp', 'row')), parts along dimension 0, may hold values from -6 to 6
- cotangent: bfloat16 [4096, 3072], P(('grp', 'row')), parts along dimension 0, may hold values from -6 to 6
- w1_blocks: bfloat16 [16, 128, 128], P('row'), may hold values from -0.5 to 0.5
- w1_rows: int32 [16], replicated, may hold values from 0 to 23
- w1_cols: int32 [16], replicated, may hold values from 0 to 95
- w2_blocks: bfloat16 [16, 128, 128], P('row'), may hold values from -0.5 to 0.5
- w2_rows: int32 [16], replicated, may hold values from 0 to 95
- w2_cols: int32 [16], replicated, may hold values from 0 to 23
Outputs:
- output: bfloat16 [4096, 3072], P(('grp', 'row')), parts along dimension 0
- input_grad: bfloat16 [4096, 3072], P(('grp', 'row')), parts along dimension 0
- w1_grad: float32 [32, 128, 128], P(('grp', 'row')), parts along dimension 0
- w2_grad: float32 [32, 128, 128], P(('grp', 'row')), parts along dimension 0
The draws below stay inside these ranges and needn't reach their ends.
There are 2 independent parts, one for each index of `grp`. The reference program is written for one: setup_inputs(seed, part) draws one part's arguments, and reference() takes and returns one part's arrays. A program takes and returns all parts, laid end to end along the dimension named above; an argument that names none is the same for every part. Nothing has to cross between parts.
All inputs are finite; a program needn't handle non-finite values.
Results may differ from the reference program's by a relative error of at most 0.005.
Values may be sent and summed in bfloat16 or wider, within the bound.
No kernel may reach another device: no remote copies, remote signals or barrier semaphores. Data moves between devices by JAX's collectives and lax.ppermute only.
A program may use at most 128 MiB of HBM per device.

```python
import jax
import jax.numpy as jnp
from jax import lax

D = 3072
BS = 128
TOK_DEV = 128
DB = 24
FB = 96
NB = 16
TOKENS = 2048


def place_ends(entries, key, smallest, top_value):
    extent = entries.shape
    index_at = [jax.random.randint(jax.random.fold_in(key, axis), (), 0, extent[axis]) for axis in range(len(extent))]
    entries = entries.at[tuple(index_at)].set(smallest)
    longest = extent.index(max(extent))
    index_at[longest] = (index_at[longest] + 1) % extent[longest]
    return entries.at[tuple(index_at)].set(top_value)


def steps_of(stream_key, extent, shards, low, largest):
    gain = 1.0
    for dim, parts in shards:
        heights = jax.random.uniform(jax.random.fold_in(jax.random.fold_in(stream_key, 6), dim), (parts,), jnp.float32, low / len(shards), largest / len(shards))
        gain = gain * jnp.repeat(jnp.exp(heights), extent[dim] // parts).reshape((-1,) + (1,) * (len(extent) - 1 - dim))
    return gain


def bell_draw(key, shape, deviation, bound, pieces=(), held_as=jnp.bfloat16):
    entries = jax.random.normal(key, shape, jnp.float32) * deviation
    if len(pieces) > 0:
        entries = steps_of(key, shape, pieces, -0.22, 0.18) * entries
    return jnp.clip(entries, min=-bound, max=bound).astype(held_as)


def setup_inputs(seed: int = 0, part: int = 0) -> dict:
    keys = jax.random.split(jax.random.key(seed), 9)
    own_keys = jax.random.split(jax.random.fold_in(keys[8], part), 9)
    tokens = bell_draw(own_keys[0], (TOKENS, D), 1.0, 6.0, ((0, 16),))
    cotangent = bell_draw(own_keys[1], (TOKENS, D), 1.0, 6.0, ((0, 16),))
    w1_blocks = bell_draw(keys[2], (NB, BS, BS), BS ** -0.5, 0.5, ((0, 16),))
    w1_rows = place_ends(jax.random.randint(keys[3], (NB,), 0, DB), jax.random.fold_in(keys[3], 1), 0, DB - 1).astype(jnp.int32)
    w1_cols = place_ends(jax.random.randint(keys[4], (NB,), 0, FB), jax.random.fold_in(keys[4], 1), 0, FB - 1).astype(jnp.int32)
    w2_blocks = bell_draw(keys[5], (NB, BS, BS), BS ** -0.5, 0.5, ((0, 16),))
    w2_rows = place_ends(jax.random.randint(keys[6], (NB,), 0, FB), jax.random.fold_in(keys[6], 1), 0, FB - 1).astype(jnp.int32)
    w2_cols = place_ends(jax.random.randint(keys[7], (NB,), 0, DB), jax.random.fold_in(keys[7], 1), 0, DB - 1).astype(jnp.int32)
    return dict(tokens=tokens, cotangent=cotangent, w1_blocks=w1_blocks, w1_rows=w1_rows, w1_cols=w1_cols, w2_blocks=w2_blocks, w2_rows=w2_rows, w2_cols=w2_cols)


def gelu_tanh(value):
    return jax.nn.gelu(value, approximate=True)

def reference(tokens, cotangent, w1_blocks, w1_rows, w1_cols, w2_blocks, w2_rows, w2_cols):
    first = w1_blocks.astype(jnp.float32)
    second = w2_blocks.astype(jnp.float32)
    count = TOKENS // TOK_DEV

    def step(carry, pair):
        grad_one, grad_two = carry
        token_rows, cot_rows = pair
        width = token_rows.shape[0]
        token_panels = token_rows.reshape(width, DB, BS).transpose(1, 0, 2).astype(jnp.float32)
        cot_panels = cot_rows.reshape(width, DB, BS).transpose(1, 0, 2).astype(jnp.float32)
        hidden = jnp.zeros((FB, width, BS), jnp.float32).at[w1_cols].add(jnp.einsum('ntk,nkj->ntj', token_panels[w1_rows], first))
        act = gelu_tanh(hidden).astype(jnp.bfloat16).astype(jnp.float32)
        output = jnp.zeros((DB, width, BS), jnp.float32).at[w2_cols].add(jnp.einsum('ntk,nkj->ntj', act[w2_rows], second))
        act_grad = jnp.zeros((FB, width, BS), jnp.float32).at[w2_rows].add(jnp.einsum('ntj,nkj->ntk', cot_panels[w2_cols], second))
        hidden_grad = jax.vjp(gelu_tanh, hidden)[1](act_grad)[0].astype(jnp.bfloat16).astype(jnp.float32)
        input_grad = jnp.zeros((DB, width, BS), jnp.float32).at[w1_rows].add(jnp.einsum('ntj,nkj->ntk', hidden_grad[w1_cols], first))
        grad_one = grad_one + jnp.einsum('ntk,ntj->nkj', token_panels[w1_rows], hidden_grad[w1_cols])
        grad_two = grad_two + jnp.einsum('ntk,ntj->nkj', act[w2_rows], cot_panels[w2_cols])
        out_rows = output.transpose(1, 0, 2).reshape(width, D).astype(jnp.bfloat16)
        grad_rows = input_grad.transpose(1, 0, 2).reshape(width, D).astype(jnp.bfloat16)
        return ((grad_one, grad_two), (out_rows, grad_rows))
    start = (jnp.zeros((NB, BS, BS), jnp.float32), jnp.zeros((NB, BS, BS), jnp.float32))
    pairs = (tokens.reshape(count, TOK_DEV, D), cotangent.reshape(count, TOK_DEV, D))
    (grad_one, grad_two), (outputs, grads) = lax.scan(step, start, pairs)
    scale = 1.0 / jnp.sqrt(jnp.float32(TOKENS))
    return (outputs.reshape(TOKENS, D), grads.reshape(TOKENS, D), grad_one * scale, grad_two * scale)
```

```python
import functools
import math

import jax
import jax.numpy as jnp
from jax import lax
from jax.experimental import pallas as pl
from jax.experimental.pallas import tpu as pltpu
from jax.sharding import PartitionSpec as P

FB = 96
ROOT = math.sqrt(2.0 / math.pi)
CUBE = 0.044715
F32 = jnp.float32
BF16 = jnp.bfloat16
VMEM = pl.BlockSpec(memory_space=pltpu.VMEM)
SMEM = pl.BlockSpec(memory_space=pltpu.SMEM)


def stages(n):
    bits = [1 << i for i in range(1, n.bit_length() - 1)]
    rounds = []
    if len(bits) % 2:
        rounds.append([bits.pop(0) | 1])
    while bits:
        low, high = bits.pop(0), bits.pop(0)
        rounds.append([low | 1, high | 1, low | high | 1])
    return rounds[::-1] + [[1]]


def slots(n):
    order = [0]
    for masks in stages(n):
        order = order + [o ^ m for m in masks for o in order]
    return order


def swap(value, mask, n):
    return lax.ppermute(value, "row", [(i, i ^ mask) for i in range(n)])


def panel(ref, index, size):
    return ref[:, pl.ds(pl.multiple_of(index * size, size), size)]


def dot(a, b, dims):
    return lax.dot_general(a, b, (dims, ((), ())), preferred_element_type=F32)


def tanh_of(v):
    return jnp.tanh(ROOT * (v + CUBE * (v * v * v)))


def gelu(v):
    return 0.5 * v * (1.0 + tanh_of(v))


def gelu_slope(v):
    t = tanh_of(v)
    return 0.5 * (1.0 + t) + 0.5 * v * (1.0 - t * t) * (ROOT * (1.0 + 3.0 * CUBE * (v * v)))


def each(count, run):
    if count <= 16:
        for s in range(count):
            run(s)
    else:
        def step(s, _):
            run(s)
            return 0
        lax.fori_loop(0, count, step, 0)


class Lists:
    def __init__(self, me, order, r1, c1, r2, c2):
        self.block = lambda s: me[0] ^ order[s]
        self.r1 = lambda s: r1[self.block(s)]
        self.c1 = lambda s: c1[self.block(s)]
        self.r2 = lambda s: r2[self.block(s)]
        self.c2 = lambda s: c2[self.block(s)]


def middle(nb, nw, me, order, r1, c1, r2, c2, tokens, cot, *refs):
    weights, (act, hgrad, send, keep, hidden, agrad) = refs[:nw], refs[nw:]
    at = Lists(me, order, r1, c1, r2, c2)
    size = act.shape[-1]
    half = nb // 2

    def w(s, which):
        return weights[s][which] if nw > 1 else weights[0][s, which]

    def clear(s):
        zero = jnp.zeros(hidden.shape[1:], F32)
        for index in (at.c1(s), at.r2(s)):
            hidden[index] = zero
            agrad[index] = zero

    each(nb, clear)

    def first(s):
        hidden[at.c1(s)] += dot(panel(tokens, at.r1(s), size), w(s, 0), ((1,), (0,)))

    each(nb, first)

    def second(s):
        agrad[at.r2(s)] += dot(panel(cot, at.c2(s), size), w(s, 1), ((1,), (1,)))

    each(nb, second)

    def slope(s):
        c = at.c1(s)
        hgrad[s] = (agrad[c] * gelu_slope(hidden[c])).astype(BF16)

    def activate(s):
        act[s] = gelu(hidden[at.r2(s)]).astype(BF16)

    def put(s, which, value):
        if isinstance(s, int):
            if s >= half:
                send[s - half, which] = value.astype(BF16)
            else:
                keep[s, which] = value
        else:
            @pl.when(s >= half)
            def _():
                send[s - half, which] = value.astype(BF16)

            @pl.when(s < half)
            def _():
                keep[s, which] = value

    def grads(s):
        activate(s)
        slope(s)
        put(s, 0, dot(panel(tokens, at.r1(s), size), hgrad[s], ((0,), (0,))))
        put(s, 1, dot(act[s], panel(cot, at.c2(s), size), ((0,), (0,))))

    each(nb, grads)


def last(nb, nw, me, order, r1, c1, r2, c2, act, hgrad, *refs):
    weights, (out, igrad, oacc, iacc) = refs[:nw], refs[nw:]
    at = Lists(me, order, r1, c1, r2, c2)
    size = act.shape[-1]

    def w(s, which):
        return weights[s][which] if nw > 1 else weights[0][s, which]

    oacc[...] = jnp.zeros_like(oacc)
    iacc[...] = jnp.zeros_like(iacc)

    def one(s):
        oacc[at.c2(s)] += dot(act[s], w(s, 1), ((1,), (0,)))
        iacc[at.r1(s)] += dot(hgrad[s], w(s, 0), ((1,), (1,)))

    each(nb, one)
    for d in range(oacc.shape[0]):
        out[:, d * size:(d + 1) * size] = oacc[d].astype(BF16)
        igrad[:, d * size:(d + 1) * size] = iacc[d].astype(BF16)


def fold(parts, scale, held, *refs):
    arrived, kept, sends = refs[:-parts], refs[-parts], refs[len(refs) - parts + 1:]
    count = kept.shape[0]

    def total(s):
        value = held[s]
        for a in arrived:
            value = value + a[s].astype(F32)
        return value

    def keep(s):
        kept[s] = total(s) * scale

    each(count, keep)
    for i, out in enumerate(sends):
        def leave(s, i=i, out=out):
            out[s] = total(count * (i + 1) + s).astype(BF16)

        each(count, leave)


def call(kernel, outs, smem, args, scratch=(), flops=0, name=None):
    size = sum(math.prod(a.shape) * a.dtype.itemsize for a in (*args, *outs))
    size += sum(math.prod(s.shape) * 4 for s in scratch)
    return pl.pallas_call(
        kernel,
        out_shape=outs,
        in_specs=[SMEM] * len(smem) + [VMEM] * len(args),
        out_specs=[VMEM] * len(outs),
        scratch_shapes=list(scratch),
        compiler_params=pltpu.CompilerParams(vmem_limit_bytes=min(size + (8 << 20), 60 << 20)),
        cost_estimate=pl.CostEstimate(flops=flops, bytes_accessed=size, transcendentals=0),
        name=name,
    )(*smem, *args)


def body(tokens, cotangent, w1_blocks, w1_rows, w1_cols, w2_blocks, w2_rows, w2_cols):
    n = lax.axis_size("row")
    nb = w1_rows.shape[0]
    width, depth = tokens.shape
    size = w1_blocks.shape[-1]
    order = slots(n)
    rounds = stages(n)
    half = nb // 2
    me = lax.axis_index("row").astype(jnp.int32).reshape(1)

    pieces = [jnp.concatenate([w1_blocks, w2_blocks], 0)]
    for masks in rounds:
        pieces = pieces + [swap(p, m, n) for m in masks for p in pieces]
    weights = pieces if n <= 16 else [jnp.stack(pieces)]
    nw = len(weights)
    if n <= 16:
        lists = (me, w1_rows, w1_cols, w2_rows, w2_cols)

        def bind(kernel):
            return lambda me, r1, c1, r2, c2, *refs: kernel(nb, nw, me, order, r1, c1, r2, c2, *refs)
    else:
        lists = (me, jnp.asarray(order, jnp.int32), w1_rows, w1_cols, w2_rows, w2_cols)

        def bind(kernel):
            return functools.partial(kernel, nb, nw)

    panels = jax.ShapeDtypeStruct((nb, width, size), BF16)
    work = 2 * nb * width * size * size
    act, hgrad, send, keep = call(
        bind(middle),
        [
            panels,
            panels,
            jax.ShapeDtypeStruct((half, 2, size, size), BF16),
            jax.ShapeDtypeStruct((half, 2, size, size), F32),
        ],
        lists,
        [tokens, cotangent, *weights],
        [pltpu.VMEM((FB, width, size), F32), pltpu.VMEM((FB, width, size), F32)],
        4 * work,
        "middle",
    )
    model = jax.ShapeDtypeStruct((width, depth), BF16)
    total = pltpu.VMEM((depth // size, width, size), F32)
    output, input_grad = call(bind(last), [model, model], lists, [act, hgrad, *weights], [total, total], 2 * work, "last")

    scale = 1.0 / math.sqrt(width * n)
    sends = [send]
    for now, later in zip(rounds[::-1], [*rounds[-2::-1], []]):
        arrived = [swap(s, m, n) for s, m in zip(sends, now)]
        parts = len(later) + 1
        count = keep.shape[0] // parts
        shape = (count, 2, size, size)
        keep, *sends = call(
            functools.partial(fold, parts, 1.0 if later else scale),
            [jax.ShapeDtypeStruct(shape, F32)] + [jax.ShapeDtypeStruct(shape, BF16)] * len(later),
            (),
            [keep, *arrived],
            (),
            0,
            "fold",
        )
    return (output, input_grad, keep[:, 0], keep[:, 1])


def solution(mesh):
    rows, blocks = P(("grp", "row"), None), P(("grp", "row"), None, None)
    return jax.shard_map(
        body,
        mesh=mesh,
        in_specs=(rows, rows, P("row", None, None), P(), P(), P("row", None, None), P(), P()),
        out_specs=(rows, rows, blocks, blocks),
        check_vma=False,
    )
```

```python
import functools
import math

import jax
import jax.numpy as jnp
from jax import lax
from jax.experimental import pallas as pl
from jax.experimental.pallas import tpu as pltpu
from jax.sharding import PartitionSpec as P

FB = 96
ROOT = math.sqrt(2.0 / math.pi)
CUBE = 0.044715
F32 = jnp.float32
BF16 = jnp.bfloat16
VMEM = pl.BlockSpec(memory_space=pltpu.VMEM)
ANY = pl.BlockSpec(memory_space=pl.ANY)
SMEM = pl.BlockSpec(memory_space=pltpu.SMEM)


def stages(n):
    bits = [1 << i for i in range(1, n.bit_length() - 1)]
    rounds = []
    if len(bits) % 2:
        rounds.append([bits.pop(0) | 1])
    while bits:
        low, high = bits.pop(0), bits.pop(0)
        rounds.append([low | 1, high | 1, low | high | 1])
    return rounds[::-1] + [[1]]


def slots(n):
    order = [0]
    for masks in stages(n):
        order = order + [o ^ m for m in masks for o in order]
    return order


def swap(value, mask, n):
    return lax.ppermute(value, "row", [(i, i ^ mask) for i in range(n)])


def panel(ref, index, size):
    return ref[:, pl.ds(pl.multiple_of(index * size, size), size)]


def dot(a, b, dims):
    return lax.dot_general(a, b, (dims, ((), ())), preferred_element_type=F32)


def tanh_of(v):
    return jnp.tanh(ROOT * (v + CUBE * (v * v * v)))


def gelu(v):
    return 0.5 * v * (1.0 + tanh_of(v))


def gelu_slope(v):
    t = tanh_of(v)
    return 0.5 * (1.0 + t) + 0.5 * v * (1.0 - t * t) * (ROOT * (1.0 + 3.0 * CUBE * (v * v)))


def each(count, run):
    if count <= 16:
        for s in range(count):
            run(s)
    else:
        def step(s, _):
            run(s)
            return 0
        lax.fori_loop(0, count, step, 0)


class Lists:
    def __init__(self, me, order, r1, c1, r2, c2):
        self.block = lambda s: me[0] ^ order[s]
        self.r1 = lambda s: r1[self.block(s)]
        self.c1 = lambda s: c1[self.block(s)]
        self.r2 = lambda s: r2[self.block(s)]
        self.c2 = lambda s: c2[self.block(s)]


def middle(nb, nw, parts, me, order, r1, c1, r2, c2, tokens, cot, *refs):
    weights, (act, hgrad, *out), (hidden, agrad, tok, ct, sems) = refs[:nw], refs[nw:-5], refs[-5:]
    sends, keeps = out[:parts], out[parts:]
    at = Lists(me, order, r1, c1, r2, c2)
    size = act.shape[-1]
    rest = nb // parts
    half = rest // 2

    def w(s, which):
        return weights[s][which] if nw > 1 else weights[0][s, which]

    def begin(s):
        pltpu.make_async_copy(panel(tokens.at, at.r1(s), size), tok.at[s], sems.at[0]).start()
        pltpu.make_async_copy(panel(cot.at, at.c2(s), size), ct.at[s], sems.at[1]).start()

    each(nb, begin)

    def clear(s):
        zero = jnp.zeros(hidden.shape[1:], F32)
        for index in (at.c1(s), at.r2(s)):
            hidden[index] = zero
            agrad[index] = zero

    each(nb, clear)

    pltpu.make_async_copy(tok, tok, sems.at[0]).wait()

    def first(s):
        hidden[at.c1(s)] += dot(tok[s], w(s, 0), ((1,), (0,)))

    each(nb, first)
    pltpu.make_async_copy(ct, ct, sems.at[1]).wait()

    def second(s):
        agrad[at.r2(s)] += dot(ct[s], w(s, 1), ((1,), (1,)))

    each(nb, second)

    def slope(s):
        c = at.c1(s)
        hgrad[s] = (agrad[c] * gelu_slope(hidden[c])).astype(BF16)

    def activate(s):
        act[s] = gelu(hidden[at.r2(s)]).astype(BF16)

    def put(i, q, which, value):
        def leave():
            sends[i][q - half, which] = value.astype(BF16)

        def stay():
            keeps[i][q, which] = value

        if isinstance(q, int):
            leave() if q >= half else stay()
        else:
            pl.when(q >= half)(leave)
            pl.when(q < half)(stay)

    def grads(i, q):
        s = i + parts * q
        activate(s)
        slope(s)
        put(i, q, 0, dot(tok[s], hgrad[s], ((0,), (0,))))
        put(i, q, 1, dot(act[s], ct[s], ((0,), (0,))))

    for i in range(parts):
        each(rest, functools.partial(grads, i))


def last(nb, nw, me, order, r1, c1, r2, c2, act, hgrad, *refs):
    weights, (out, igrad, oacc, iacc) = refs[:nw], refs[nw:]
    at = Lists(me, order, r1, c1, r2, c2)
    size = act.shape[-1]

    def w(s, which):
        return weights[s][which] if nw > 1 else weights[0][s, which]

    oacc[...] = jnp.zeros_like(oacc)
    iacc[...] = jnp.zeros_like(iacc)

    def one(s):
        oacc[at.c2(s)] += dot(act[s], w(s, 1), ((1,), (0,)))
        iacc[at.r1(s)] += dot(hgrad[s], w(s, 0), ((1,), (1,)))

    each(nb, one)
    for d in range(oacc.shape[0]):
        out[:, d * size:(d + 1) * size] = oacc[d].astype(BF16)
        igrad[:, d * size:(d + 1) * size] = iacc[d].astype(BF16)


def fold(parts, held, *refs):
    arrived, outs = refs[:-parts], refs[-parts:]
    count = outs[0].shape[0]
    for i, out in enumerate(outs):
        def one(q, i=i, out=out):
            value = held[count * i + q]
            for a in arrived:
                value = value + a[count * i + q].astype(F32)
            out[q] = value.astype(out.dtype)

        each(count, one)


def close(scale, held, *refs):
    arrived, outs = refs[:-2], refs[-2:]
    for which, out in enumerate(outs):
        value = held[0, which]
        for a in arrived:
            value = value + a[0, which].astype(F32)
        out[0] = value * scale


def call(kernel, outs, smem, args, scratch=(), flops=0, name=None, any_args=()):
    size = sum(math.prod(a.shape) * a.dtype.itemsize for a in (*args, *outs))
    size += sum(math.prod(s.shape) * 4 for s in scratch[:4])
    return pl.pallas_call(
        kernel,
        out_shape=outs,
        in_specs=[SMEM] * len(smem) + [ANY] * len(any_args) + [VMEM] * len(args),
        out_specs=[VMEM] * len(outs),
        scratch_shapes=list(scratch),
        compiler_params=pltpu.CompilerParams(vmem_limit_bytes=min(size + (4 << 20), 60 << 20)),
        cost_estimate=pl.CostEstimate(flops=flops, bytes_accessed=size, transcendentals=0),
        name=name,
    )(*smem, *[pltpu.with_memory_space_constraint(a, pltpu.HBM) for a in any_args], *args)


def body(tokens, cotangent, w1_blocks, w1_rows, w1_cols, w2_blocks, w2_rows, w2_cols):
    n = lax.axis_size("row")
    nb = w1_rows.shape[0]
    width, depth = tokens.shape
    size = w1_blocks.shape[-1]
    order = slots(n)
    rounds = stages(n)
    me = lax.axis_index("row").astype(jnp.int32).reshape(1)

    pieces = [jnp.concatenate([w1_blocks, w2_blocks], 0)]
    for masks in rounds:
        pieces = pieces + [swap(p, m, n) for m in masks for p in pieces]
    weights = pieces if n <= 16 else [jnp.stack(pieces)]
    nw = len(weights)
    if n <= 16:
        lists = (me, w1_rows, w1_cols, w2_rows, w2_cols)

        def bind(kernel, *given):
            return lambda me, r1, c1, r2, c2, *refs: kernel(*given, me, order, r1, c1, r2, c2, *refs)
    else:
        lists = (me, jnp.asarray(order, jnp.int32), w1_rows, w1_cols, w2_rows, w2_cols)

        def bind(kernel, *given):
            return functools.partial(kernel, *given)

    def blocks(count, dtype):
        return jax.ShapeDtypeStruct((count, 2, size, size), dtype)

    parts = len(rounds[0]) + 1
    half = nb // parts // 2
    panels = jax.ShapeDtypeStruct((nb, width, size), BF16)
    work = 2 * nb * width * size * size
    act, hgrad, *out = call(
        bind(middle, nb, nw, parts),
        [panels, panels] + [blocks(half, BF16)] * parts + [blocks(half, F32)] * parts,
        lists,
        weights,
        [
            pltpu.VMEM((FB, width, size), F32),
            pltpu.VMEM((FB, width, size), F32),
            pltpu.VMEM((nb, width, size), BF16),
            pltpu.VMEM((nb, width, size), BF16),
            pltpu.SemaphoreType.DMA((2,)),
        ],
        4 * work,
        "middle",
        (tokens, cotangent),
    )
    model = jax.ShapeDtypeStruct((width, depth), BF16)
    total = pltpu.VMEM((depth // size, width, size), F32)
    output, input_grad = call(bind(last, nb, nw), [model, model], lists, [act, hgrad, *weights], [total, total], 2 * work, "last")

    sends, keeps = out[:parts], out[parts:]
    near = rounds[1:][::-1]
    landed = []
    for i in range(parts):
        leaving, held = [sends[i]], keeps[i]
        for now, later in zip(near, [*near[1:], []]):
            arrived = [swap(v, m, n) for v, m in zip(leaving, now)]
            if later or i:
                count = held.shape[0] // (len(later) + 1)
                kept = blocks(count, F32 if later else BF16)
                held, *leaving = call(
                    functools.partial(fold, len(later) + 1),
                    [kept] + [blocks(count, BF16)] * len(later),
                    (),
                    [held, *arrived],
                    name="fold",
                )
        landed += [held, *arrived] if i == 0 else [swap(held, rounds[0][i - 1], n)]
    grad = jax.ShapeDtypeStruct((1, size, size), F32)
    first_grad, second_grad = call(
        functools.partial(close, 1.0 / math.sqrt(width * n)), [grad, grad], (), landed, name="close"
    )
    return (output, input_grad, first_grad, second_grad)


def solution(mesh):
    rows, blocks = P(("grp", "row"), None), P(("grp", "row"), None, None)
    return jax.shard_map(
        body,
        mesh=mesh,
        in_specs=(rows, rows, P("row", None, None), P(), P(), P("row", None, None), P(), P()),
        out_specs=(rows, rows, blocks, blocks),
        check_vma=False,
    )
```

```python
import functools
import math

import jax
import jax.numpy as jnp
from jax import lax
from jax.experimental import pallas as pl
from jax.experimental.pallas import tpu as pltpu
from jax.sharding import PartitionSpec as P

FB = 96
BEGIN_FLOPS = 10**10
CHUNK = 6
PRE_SLOT = 3
TIE = 1
EARLY = 4
ROOT = math.sqrt(2.0 / math.pi)
CUBE = 0.044715
F32 = jnp.float32
BF16 = jnp.bfloat16
VMEM = pl.BlockSpec(memory_space=pltpu.VMEM)
ANY = pl.BlockSpec(memory_space=pl.ANY)
SMEM = pl.BlockSpec(memory_space=pltpu.SMEM)


GATHER = [[9, 5, 13], [3], [1]]
EXCHANGE = [[9, 5, 13], [3], [1]]


def bits(n):
    return [(1 << i) | 1 for i in range(n.bit_length() - 2, 0, -1)]


def gather_rounds(n):
    if GATHER and n == 16:
        return GATHER
    return [[b] for b in bits(n)] + [[1]]


def exchange_rounds(n):
    if EXCHANGE and n == 16:
        return EXCHANGE
    far, rounds = bits(n), []
    while far:
        a, far = far[0], far[1:]
        masks = [a]
        if far:
            b, far = far[0], far[1:]
            masks = [a, b, a ^ b]
        rounds.append(masks)
    return rounds + [[1]]


def slots(rounds):
    order = [0]
    for masks in rounds:
        order = order + [o ^ m for m in masks for o in order]
    return order


def swap(value, mask, n):
    return lax.ppermute(value, "row", [(i, i ^ mask) for i in range(n)])


def panel(ref, index, size):
    return ref[:, pl.ds(pl.multiple_of(index * size, size), size)]


def dot(a, b, dims):
    return lax.dot_general(a, b, (dims, ((), ())), preferred_element_type=F32)


def tanh_of(v, u):
    return jnp.tanh(v * (ROOT + ROOT * CUBE * u))


def gelu(v):
    h = 0.5 * v
    return h + h * tanh_of(v, v * v)


def gelu_slope(v):
    u = v * v
    t = tanh_of(v, u)
    g = 0.5 + 0.5 * t
    return g + (g * (1.0 - t)) * (v * (ROOT + 3.0 * ROOT * CUBE * u))


def each(count, run):
    if count <= 16:
        for s in range(count):
            run(s)
    else:
        def step(s, _):
            run(s)
            return 0
        lax.fori_loop(0, count, step, 0)


class Lists:
    def __init__(self, me, order, r1, c1, r2, c2):
        self.block = lambda s: me[0] ^ order[s]
        self.r1 = lambda s: r1[self.block(s)]
        self.c1 = lambda s: c1[self.block(s)]
        self.r2 = lambda s: r2[self.block(s)]
        self.c2 = lambda s: c2[self.block(s)]


def begin(w1, w2, weights, sems):
    copies = [
        pltpu.make_async_copy(w1, weights.at[pl.ds(0, 1)], sems.at[0]),
        pltpu.make_async_copy(w2, weights.at[pl.ds(1, 1)], sems.at[1]),
    ]
    for copy in copies:
        copy.start()
    for copy in copies:
        copy.wait()


def middle(nb, nw, parts, place, me, order, r1, c1, r2, c2, tokens, cot, *refs):
    weights, (act, hgrad, *out), (hidden, agrad) = refs[:nw], refs[nw:-2], refs[-2:]
    sends, keeps = out[:parts], out[parts:]
    at = Lists(me, order, r1, c1, r2, c2)
    size = act.shape[-1]
    rest = nb // parts
    half = rest // 2

    def w(s, which):
        return weights[s][which] if nw > 1 else weights[0][s, which]

    def clear(s):
        zero = jnp.zeros(hidden.shape[1:], F32)
        for index in (at.c1(s), at.r2(s)):
            hidden[index] = zero
            agrad[index] = zero

    each(nb, clear)


    def first(s):
        hidden[at.c1(s)] += dot(panel(tokens, at.r1(s), size), w(s, 0), ((1,), (0,)))

    each(nb, first)

    def second(s):
        agrad[at.r2(s)] += dot(panel(cot, at.c2(s), size), w(s, 1), ((1,), (1,)))

    each(nb, second)

    def slope(s):
        c = at.c1(s)
        hgrad[s] = (agrad[c] * gelu_slope(hidden[c])).astype(BF16)

    def activate(s):
        act[s] = gelu(hidden[at.r2(s)]).astype(BF16)

    def put(i, q, which, value):
        def leave():
            sends[i][q - half, which] = value.astype(BF16)

        def stay():
            keeps[i][q, which] = value

        if isinstance(q, int):
            leave() if q >= half else stay()
        else:
            pl.when(q >= half)(leave)
            pl.when(q < half)(stay)

    def grads(i, q):
        s = i + parts * q
        s = place[s] if isinstance(q, int) else s
        activate(s)
        slope(s)
        put(i, q, 0, dot(panel(tokens, at.r1(s), size), hgrad[s], ((0,), (0,))))
        put(i, q, 1, dot(act[s], panel(cot, at.c2(s), size), ((0,), (0,))))

    for i in range(parts):
        each(rest, functools.partial(grads, i))


def finish(nb, table, act, hgrad, *refs):
    weights, (out, igrad, oacc, iacc, ostage, istage, sems) = refs[:nb], refs[nb:]
    size = act.shape[-1]
    count = oacc.shape[0]
    oacc[...] = jnp.zeros_like(oacc)
    iacc[...] = jnp.zeros_like(iacc)
    for s in range(nb):
        oacc[table[3, s]] += dot(act[s], weights[s][1], ((1,), (0,)))
        iacc[table[2, s]] += dot(hgrad[s], weights[s][0], ((1,), (1,)))
    copies = []
    for acc, stage, target in ((oacc, ostage, out), (iacc, istage, igrad)):
        for d in range(0, count, CHUNK):
            for e in range(d, d + CHUNK):
                stage[:, e * size:(e + 1) * size] = acc[e].astype(BF16)
            at = (slice(None), pl.ds(d * size, CHUNK * size))
            copies.append(pltpu.make_async_copy(stage.at[at], target.at[at], sems.at[len(copies)]))
            copies[-1].start()
    for copy in copies:
        copy.wait()


def ready(nb, order, me, r1, c1, r2, c2, tokens, cot, piece, *refs):
    weights, (passed, hidden, agrad, tok, tok_t, ct, ct_t, table) = refs[:-8], refs[-8:]
    del piece, passed
    at = Lists(me, order, r1, c1, r2, c2)
    size = tok.shape[-1]
    zero = jnp.zeros(hidden.shape[1:], F32)
    for s in range(nb):
        hidden[at.c1(s)] = zero
        hidden[at.r2(s)] = zero
        agrad[at.c1(s)] = zero
        agrad[at.r2(s)] = zero
    lane = lax.broadcasted_iota(jnp.int32, table.shape, 1)
    row = lax.broadcasted_iota(jnp.int32, table.shape, 0)
    entries = jnp.zeros(table.shape, jnp.int32)
    for s in range(nb):
        value = jnp.where(row < 2, jnp.where(row == 0, at.c1(s), at.r2(s)), jnp.where(row == 2, at.r1(s), at.c2(s)))
        entries = jnp.where(lane == s, value, entries)
    table[...] = entries
    for s in range(nb):
        value = panel(tokens, at.r1(s), size)
        tok[s] = value
        tok_t[s] = value.T
        value = panel(cot, at.c2(s), size)
        ct[s] = value
        ct_t[s] = value.T
    for s, w in enumerate(weights):
        hidden[at.c1(s)] += dot(tok[s], w[0], ((1,), (0,)))
        agrad[at.r2(s)] += dot(ct[s], w[1], ((1,), (1,)))


def core(nb, parts, place, table, hidden_in, agrad_in, tok, tok_t, ct, ct_t, *refs):
    late, (hidden, agrad, act, hgrad, *out, prod, prod_t) = refs[:-6 - 2 * parts], refs[-6 - 2 * parts:]
    del hidden_in, agrad_in
    sends, keeps = out[:parts], out[parts:]
    ne = nb - len(late)
    for i, w in enumerate(late):
        prod[i] = dot(tok[ne + i], w[0], ((1,), (0,)))
        prod_t[i] = dot(ct[ne + i], w[1], ((1,), (1,)))
    c1 = [table[0, s] for s in range(nb)]
    r2 = [table[1, s] for s in range(nb)]
    for i in range(len(late)):
        hidden[c1[ne + i]] += prod[i]
    for i in range(len(late)):
        agrad[r2[ne + i]] += prod_t[i]
    half = nb // parts // 2

    def put(e, which, value):
        i, q = e % parts, e // parts
        if q < half:
            keeps[i][q, which] = value
        else:
            sends[i][q - half, which] = value.astype(BF16)

    for s in range(nb):
        act[s] = gelu(hidden[r2[s]]).astype(BF16)
        hgrad[s] = (agrad[c1[s]] * gelu_slope(hidden[c1[s]])).astype(BF16)
    for e, s in enumerate(place):
        put(e, 0, dot(tok_t[s], hgrad[s], ((1,), (0,))))
        put(e, 1, dot(ct_t[s], act[s], ((1,), (0,))))


def last(nb, nw, me, order, r1, c1, r2, c2, act, hgrad, *refs):
    weights, (out, igrad, oacc, iacc) = refs[:nw], refs[nw:]
    at = Lists(me, order, r1, c1, r2, c2)
    size = act.shape[-1]

    def w(s, which):
        return weights[s][which] if nw > 1 else weights[0][s, which]

    oacc[...] = jnp.zeros_like(oacc)
    iacc[...] = jnp.zeros_like(iacc)

    def one(s):
        oacc[at.c2(s)] += dot(act[s], w(s, 1), ((1,), (0,)))
        iacc[at.r1(s)] += dot(hgrad[s], w(s, 0), ((1,), (1,)))

    each(nb, one)
    for d in range(oacc.shape[0]):
        out[:, d * size:(d + 1) * size] = oacc[d].astype(BF16)
        igrad[:, d * size:(d + 1) * size] = iacc[d].astype(BF16)


def fold(parts, held, *refs):
    arrived, outs = refs[:-parts], refs[-parts:]
    count = outs[0].shape[0]
    for i, out in enumerate(outs):
        def one(q, i=i, out=out):
            value = held[count * i + q]
            for a in arrived:
                value = value + a[count * i + q].astype(F32)
            out[q] = value.astype(out.dtype)

        each(count, one)


def close(scale, turned, held, *refs):
    arrived, outs = refs[:-2], refs[-2:]
    for which, out in enumerate(outs):
        value = held[0, which]
        for a in arrived:
            value = value + a[0, which].astype(F32)
        value = value * scale
        out[0] = value.T if which == turned else value


def copy_after(value, other, out):
    del other
    out[...] = value[...]


def after(value, other):
    return call(copy_after, [jax.ShapeDtypeStruct(value.shape, value.dtype)], (), [value, other], (), BEGIN_FLOPS, "after")[0]


def call(kernel, outs, smem, args, scratch=(), flops=0, name=None, hbm_args=(), any_args=(), aliases=(), hbm_outs=False):
    size = sum(math.prod(a.shape) * a.dtype.itemsize for a in (*args, *outs))
    size += sum(math.prod(s.shape) * 4 for s in scratch)
    first = len(smem) + len(hbm_args) + len(any_args)
    return pl.pallas_call(
        kernel,
        out_shape=outs,
        in_specs=[SMEM] * len(smem) + [ANY] * (len(hbm_args) + len(any_args)) + [VMEM] * len(args),
        out_specs=[ANY if hbm_outs else VMEM] * len(outs),
        scratch_shapes=list(scratch),
        input_output_aliases={first + i: o for i, o in aliases},
        compiler_params=pltpu.CompilerParams(vmem_limit_bytes=min(size + (4 << 20), 60 << 20)),
        cost_estimate=pl.CostEstimate(flops=flops, bytes_accessed=size, transcendentals=0),
        name=name,
    )(*smem, *[pltpu.with_memory_space_constraint(a, pltpu.HBM) for a in hbm_args], *any_args, *args)


def body(tokens, cotangent, w1_blocks, w1_rows, w1_cols, w2_blocks, w2_rows, w2_cols):
    n = lax.axis_size("row")
    nb = w1_rows.shape[0]
    width, depth = tokens.shape
    size = w1_blocks.shape[-1]
    order = slots(gather_rounds(n))
    rounds = exchange_rounds(n)
    place = [order.index(o) for o in slots(rounds)]
    me = lax.axis_index("row").astype(jnp.int32).reshape(1)

    (own,) = call(
        begin,
        [jax.ShapeDtypeStruct((2, size, size), BF16)],
        (),
        (),
        [pltpu.SemaphoreType.DMA((2,))],
        0,
        "begin",
        (w1_blocks, w2_blocks),
    )
    fast = n <= 16
    panels = jax.ShapeDtypeStruct((nb, width, size), BF16)
    units = jax.ShapeDtypeStruct((FB, width, size), F32)
    pieces = [own]
    for masks in gather_rounds(n)[:-1]:
        moving = list(pieces)
        if fast and TIE and len(pieces) > 1:
            moving[0] = after(pieces[0], pieces[TIE])
        pieces = pieces + [swap(p, m, n) for m in masks for p in moving]
    moved = list(pieces)
    if fast:
        moved[PRE_SLOT], hidden, agrad, tok, tok_t, ct, ct_t, table = call(
            functools.partial(ready, nb, order),
            [jax.ShapeDtypeStruct(own.shape, BF16), units, units, panels, panels, panels, panels, jax.ShapeDtypeStruct((8, 128), jnp.int32)],
            (me, w1_rows, w1_cols, w2_rows, w2_cols),
            [tokens, cotangent, pieces[PRE_SLOT], *pieces[:EARLY]],
            name="ready",
            aliases=((2, 0),),
        )
    pieces = pieces + [swap(p, 1, n) for p in moved]
    weights = pieces if n <= 16 else [jnp.stack(pieces)]
    nw = len(weights)
    if n <= 16:
        lists = (me, w1_rows, w1_cols, w2_rows, w2_cols)

        def bind(kernel, *given):
            return lambda me, r1, c1, r2, c2, *refs: kernel(*given, me, order, r1, c1, r2, c2, *refs)
    else:
        assert place == list(range(nb))
        lists = (me, jnp.asarray(order, jnp.int32), w1_rows, w1_cols, w2_rows, w2_cols)

        def bind(kernel, *given):
            return functools.partial(kernel, *given)

    def blocks(count, dtype):
        return jax.ShapeDtypeStruct((count, 2, size, size), dtype)

    parts = len(rounds[0]) + 1
    half = nb // parts // 2
    work = 2 * nb * width * size * size
    outs = [panels, panels] + [blocks(half, BF16)] * parts + [blocks(half, F32)] * parts
    if fast:
        late = nb - EARLY
        _, _, act, hgrad, *out = call(
            functools.partial(core, nb, parts, place),
            [units, units, *outs],
            (),
            [table, hidden, agrad, tok, tok_t, ct, ct_t, *pieces[EARLY:]],
            [
                pltpu.VMEM((late, width, size), F32),
                pltpu.VMEM((late, width, size), F32),
            ],
            4 * work,
            "middle",
            aliases=((1, 0), (2, 1)),
        )
    else:
        act, hgrad, *out = call(
            bind(middle, nb, nw, parts, place),
            outs,
            lists,
            [tokens, cotangent, *weights],
            [pltpu.VMEM((FB, width, size), F32), pltpu.VMEM((FB, width, size), F32)],
            4 * work,
            "middle",
        )
    model = jax.ShapeDtypeStruct((width, depth), BF16)
    total = pltpu.VMEM((depth // size, width, size), F32)
    if fast:
        stage = pltpu.VMEM((width, depth), BF16)
        output, input_grad = call(
            functools.partial(finish, nb),
            [model, model],
            (),
            [table, act, hgrad, *weights],
            [total, total, stage, stage, pltpu.SemaphoreType.DMA((2 * (depth // size // CHUNK),))],
            2 * work,
            "last",
            hbm_outs=True,
        )
    else:
        output, input_grad = call(bind(last, nb, nw), [model, model], lists, [act, hgrad, *weights], [total, total], 2 * work, "last")

    sends, keeps = out[:parts], out[parts:]
    near = rounds[1:][::-1]
    landed = []
    for i in range(parts):
        leaving, held = [sends[i]], keeps[i]
        for now, later in zip(near, [*near[1:], []]):
            arrived = [swap(v, m, n) for v, m in zip(leaving, now)]
            if later or i:
                count = held.shape[0] // (len(later) + 1)
                kept = blocks(count, F32 if later else BF16)
                held, *leaving = call(
                    functools.partial(fold, len(later) + 1),
                    [kept] + [blocks(count, BF16)] * len(later),
                    (),
                    [held, *arrived],
                    name="fold",
                )
        landed += [held, *arrived] if i == 0 else [swap(held, rounds[0][i - 1], n)]
    grad = jax.ShapeDtypeStruct((1, size, size), F32)
    first_grad, second_grad = call(
        functools.partial(close, 1.0 / math.sqrt(width * n), 1 if fast else -1), [grad, grad], (), landed, name="close"
    )
    return (output, input_grad, first_grad, second_grad)


def solution(mesh):
    rows, blocks = P(("grp", "row"), None), P(("grp", "row"), None, None)
    return jax.shard_map(
        body,
        mesh=mesh,
        in_specs=(rows, rows, P("row", None, None), P(), P(), P("row", None, None), P(), P()),
        out_specs=(rows, rows, blocks, blocks),
        check_vma=False,
    )
```

```python
import functools
import math

import jax
import jax.numpy as jnp
from jax import lax
from jax.experimental import pallas as pl
from jax.experimental.pallas import tpu as pltpu
from jax.sharding import PartitionSpec as P

FB = 96
BEGIN_FLOPS = 10**10
CHUNK = 6
PRE_SLOT = 3
TIE = 1
EARLY = 4
TAIL = 1
GROUPS = ((1,), (2,), (3,), (0,))
SPLIT = 0
ROOT = math.sqrt(2.0 / math.pi)
CUBE = 0.044715
F32 = jnp.float32
BF16 = jnp.bfloat16
VMEM = pl.BlockSpec(memory_space=pltpu.VMEM)
ANY = pl.BlockSpec(memory_space=pl.ANY)
SMEM = pl.BlockSpec(memory_space=pltpu.SMEM)


GATHER = [[9, 5, 13], [3], [1]]
EXCHANGE = [[9, 5, 13], [3], [1]]


def bits(n):
    return [(1 << i) | 1 for i in range(n.bit_length() - 2, 0, -1)]


def gather_rounds(n):
    if GATHER and n == 16:
        return GATHER
    return [[b] for b in bits(n)] + [[1]]


def exchange_rounds(n):
    if EXCHANGE and n == 16:
        return EXCHANGE
    far, rounds = bits(n), []
    while far:
        a, far = far[0], far[1:]
        masks = [a]
        if far:
            b, far = far[0], far[1:]
            masks = [a, b, a ^ b]
        rounds.append(masks)
    return rounds + [[1]]


def slots(rounds):
    order = [0]
    for masks in rounds:
        order = order + [o ^ m for m in masks for o in order]
    return order


def swap(value, mask, n):
    return lax.ppermute(value, "row", [(i, i ^ mask) for i in range(n)])


def panel(ref, index, size):
    return ref[:, pl.ds(pl.multiple_of(index * size, size), size)]


def dot(a, b, dims):
    return lax.dot_general(a, b, (dims, ((), ())), preferred_element_type=F32)


def tanh_of(v, u):
    return jnp.tanh(v * (ROOT + ROOT * CUBE * u))


def gelu(v):
    h = 0.5 * v
    return h + h * tanh_of(v, v * v)


def gelu_slope(v):
    u = v * v
    t = tanh_of(v, u)
    g = 0.5 + 0.5 * t
    return g + (g * (1.0 - t)) * (v * (ROOT + 3.0 * ROOT * CUBE * u))


def twice_gelu(v):
    return v + v * tanh_of(v, v * v)


def twice_gelu_slope(v):
    u = v * v
    t = tanh_of(v, u)
    p = 1.0 + t
    return p + (p * (1.0 - t)) * (v * (ROOT + 3.0 * ROOT * CUBE * u))


def each(count, run):
    if count <= 16:
        for s in range(count):
            run(s)
    else:
        def step(s, _):
            run(s)
            return 0
        lax.fori_loop(0, count, step, 0)


class Lists:
    def __init__(self, me, order, r1, c1, r2, c2):
        self.block = lambda s: me[0] ^ order[s]
        self.r1 = lambda s: r1[self.block(s)]
        self.c1 = lambda s: c1[self.block(s)]
        self.r2 = lambda s: r2[self.block(s)]
        self.c2 = lambda s: c2[self.block(s)]


def begin(w1, w2, weights, sems):
    copies = [
        pltpu.make_async_copy(w1, weights.at[pl.ds(0, 1)], sems.at[0]),
        pltpu.make_async_copy(w2, weights.at[pl.ds(1, 1)], sems.at[1]),
    ]
    for copy in copies:
        copy.start()
    for copy in copies:
        copy.wait()


def middle(nb, nw, parts, place, me, order, r1, c1, r2, c2, tokens, cot, *refs):
    weights, (act, hgrad, *out), (hidden, agrad) = refs[:nw], refs[nw:-2], refs[-2:]
    sends, keeps = out[:parts], out[parts:]
    at = Lists(me, order, r1, c1, r2, c2)
    size = act.shape[-1]
    rest = nb // parts
    half = rest // 2

    def w(s, which):
        return weights[s][which] if nw > 1 else weights[0][s, which]

    def clear(s):
        zero = jnp.zeros(hidden.shape[1:], F32)
        for index in (at.c1(s), at.r2(s)):
            hidden[index] = zero
            agrad[index] = zero

    each(nb, clear)


    def first(s):
        hidden[at.c1(s)] += dot(panel(tokens, at.r1(s), size), w(s, 0), ((1,), (0,)))

    each(nb, first)

    def second(s):
        agrad[at.r2(s)] += dot(panel(cot, at.c2(s), size), w(s, 1), ((1,), (1,)))

    each(nb, second)

    def slope(s):
        c = at.c1(s)
        hgrad[s] = (agrad[c] * gelu_slope(hidden[c])).astype(BF16)

    def activate(s):
        act[s] = gelu(hidden[at.r2(s)]).astype(BF16)

    def put(i, q, which, value):
        def leave():
            sends[i][q - half, which] = value.astype(BF16)

        def stay():
            keeps[i][q, which] = value

        if isinstance(q, int):
            leave() if q >= half else stay()
        else:
            pl.when(q >= half)(leave)
            pl.when(q < half)(stay)

    def grads(i, q):
        s = i + parts * q
        s = place[s] if isinstance(q, int) else s
        activate(s)
        slope(s)
        put(i, q, 0, dot(panel(tokens, at.r1(s), size), hgrad[s], ((0,), (0,))))
        put(i, q, 1, dot(act[s], panel(cot, at.c2(s), size), ((0,), (0,))))

    for i in range(parts):
        each(rest, functools.partial(grads, i))


def finish(nb, table, act, hgrad, *refs):
    weights, (out, igrad, oacc, iacc, ostage, istage, sems) = refs[:nb], refs[nb:]
    size = act.shape[-1]
    count = oacc.shape[0]
    oacc[...] = jnp.zeros_like(oacc)
    iacc[...] = jnp.zeros_like(iacc)
    for s in range(nb):
        oacc[table[3, s]] += dot(act[s], weights[s][1], ((1,), (0,)))
        iacc[table[2, s]] += dot(hgrad[s], weights[s][0], ((1,), (1,)))
    copies = []
    for acc, stage, target in ((oacc, ostage, out), (iacc, istage, igrad)):
        for d in range(0, count, CHUNK):
            for e in range(d, d + CHUNK):
                stage[:, e * size:(e + 1) * size] = (0.5 * acc[e]).astype(BF16)
            at = (slice(None), pl.ds(d * size, CHUNK * size))
            copies.append(pltpu.make_async_copy(stage.at[at], target.at[at], sems.at[len(copies)]))
            copies[-1].start()
    for copy in copies:
        copy.wait()


def ready(nb, order, me, r1, c1, r2, c2, tokens, cot, piece, *refs):
    weights, (passed, hidden, agrad, tok, tok_t, ct, ct_t, table) = refs[:-8], refs[-8:]
    del piece, passed
    at = Lists(me, order, r1, c1, r2, c2)
    size = tok.shape[-1]
    zero = jnp.zeros(hidden.shape[1:], F32)
    for s in range(nb):
        hidden[at.c1(s)] = zero
        hidden[at.r2(s)] = zero
        agrad[at.c1(s)] = zero
        agrad[at.r2(s)] = zero
    lane = lax.broadcasted_iota(jnp.int32, table.shape, 1)
    row = lax.broadcasted_iota(jnp.int32, table.shape, 0)
    entries = jnp.zeros(table.shape, jnp.int32)
    for s in range(nb):
        value = jnp.where(row < 2, jnp.where(row == 0, at.c1(s), at.r2(s)), jnp.where(row == 2, at.r1(s), at.c2(s)))
        entries = jnp.where(lane == s, value, entries)
    table[...] = entries
    for s in range(nb):
        value = panel(tokens, at.r1(s), size)
        tok[s] = value
        tok_t[s] = value.T
        value = panel(cot, at.c2(s), size)
        ct[s] = value
        ct_t[s] = value.T
    for s, w in enumerate(weights):
        hidden[at.c1(s)] += dot(tok[s], w[0], ((1,), (0,)))
        agrad[at.r2(s)] += dot(ct[s], w[1], ((1,), (1,)))


def add_products(late, table, tok, ct, refs, hidden, agrad, prod, prod_t):
    for i, (s, w) in enumerate(zip(late, refs)):
        prod[i] = dot(tok[s], w[0], ((1,), (0,)))
        prod_t[i] = dot(ct[s], w[1], ((1,), (1,)))
    for i, s in enumerate(late):
        hidden[table[0, s]] += prod[i]
    for i, s in enumerate(late):
        agrad[table[1, s]] += prod_t[i]


def more(late, table, hidden_in, agrad_in, tok, ct, *refs):
    weights, (hidden, agrad, prod, prod_t) = refs[:-4], refs[-4:]
    del hidden_in, agrad_in
    add_products(late, table, tok, ct, weights, hidden, agrad, prod, prod_t)


def grads_of(groups, parts, place, tok_t, ct_t, act, hgrad, out):
    sends, keeps = out[:len(groups)], out[len(groups):]
    half = len(place) // parts // 2
    for group, send, keep in zip(groups, sends, keeps):
        for q in range(2 * half):
            for k, i in enumerate(group):
                s = place[i + parts * q]
                at = q % half * len(group) + k
                values = dot(tok_t[s], hgrad[s], ((1,), (0,))), dot(ct_t[s], act[s], ((1,), (0,)))
                for which, value in enumerate(values):
                    if q < half:
                        keep[at, which] = value
                    else:
                        send[at, which] = value.astype(BF16)


def core(nb, parts, place, late, pieces, table, hidden_in, agrad_in, tok, tok_t, ct, ct_t, *refs):
    weights, (hidden, agrad, act, hgrad, *out, prod, prod_t) = refs[:len(late)], refs[len(late):]
    del hidden_in, agrad_in
    add_products(late, table, tok, ct, weights, hidden, agrad, prod, prod_t)
    for s in range(nb):
        act[s] = twice_gelu(hidden[table[1, s]]).astype(BF16)
        c = table[0, s]
        hgrad[s] = (agrad[c] * twice_gelu_slope(hidden[c])).astype(BF16)
    grads_of(pieces, parts, place, tok_t, ct_t, act, hgrad, out)


def rest(parts, place, pieces, arrived, tok_t, ct_t, act, hgrad, *out):
    del arrived
    grads_of(pieces, parts, place, tok_t, ct_t, act, hgrad, out)


def last(nb, nw, me, order, r1, c1, r2, c2, act, hgrad, *refs):
    weights, (out, igrad, oacc, iacc) = refs[:nw], refs[nw:]
    at = Lists(me, order, r1, c1, r2, c2)
    size = act.shape[-1]

    def w(s, which):
        return weights[s][which] if nw > 1 else weights[0][s, which]

    oacc[...] = jnp.zeros_like(oacc)
    iacc[...] = jnp.zeros_like(iacc)

    def one(s):
        oacc[at.c2(s)] += dot(act[s], w(s, 1), ((1,), (0,)))
        iacc[at.r1(s)] += dot(hgrad[s], w(s, 0), ((1,), (1,)))

    each(nb, one)
    for d in range(oacc.shape[0]):
        out[:, d * size:(d + 1) * size] = oacc[d].astype(BF16)
        igrad[:, d * size:(d + 1) * size] = iacc[d].astype(BF16)


def fold(parts, held, *refs):
    arrived, outs = refs[:-parts], refs[-parts:]
    count = outs[0].shape[0]
    for i, out in enumerate(outs):
        def one(q, i=i, out=out):
            value = held[count * i + q]
            for a in arrived:
                value = value + a[count * i + q].astype(F32)
            out[q] = value.astype(out.dtype)

        each(count, one)


def close(scale, turned, held, *refs):
    arrived, outs = refs[:-2], refs[-2:]
    for which, out in enumerate(outs):
        value = held[held.shape[0] - 1, which]
        for a in arrived:
            value = value + a[a.shape[0] - 1, which].astype(F32)
        value = value * scale
        out[0] = value.T if which == turned else value


def copy_after(value, other, out):
    del other
    out[...] = value[...]


def after(value, other):
    return call(copy_after, [jax.ShapeDtypeStruct(value.shape, value.dtype)], (), [value, other], (), BEGIN_FLOPS, "after")[0]


def call(kernel, outs, smem, args, scratch=(), flops=0, name=None, hbm_args=(), any_args=(), aliases=(), hbm_outs=False):
    size = sum(math.prod(a.shape) * a.dtype.itemsize for a in (*args, *outs))
    size += sum(math.prod(s.shape) * 4 for s in scratch)
    first = len(smem) + len(hbm_args) + len(any_args)
    return pl.pallas_call(
        kernel,
        out_shape=outs,
        in_specs=[SMEM] * len(smem) + [ANY] * (len(hbm_args) + len(any_args)) + [VMEM] * len(args),
        out_specs=[ANY if hbm_outs else VMEM] * len(outs),
        scratch_shapes=list(scratch),
        input_output_aliases={first + i: o for i, o in aliases},
        compiler_params=pltpu.CompilerParams(vmem_limit_bytes=min(size + (4 << 20), 60 << 20)),
        cost_estimate=pl.CostEstimate(flops=flops, bytes_accessed=size, transcendentals=0),
        name=name,
    )(*smem, *[pltpu.with_memory_space_constraint(a, pltpu.HBM) for a in hbm_args], *any_args, *args)


def body(tokens, cotangent, w1_blocks, w1_rows, w1_cols, w2_blocks, w2_rows, w2_cols):
    n = lax.axis_size("row")
    nb = w1_rows.shape[0]
    width, depth = tokens.shape
    size = w1_blocks.shape[-1]
    order = slots(gather_rounds(n))
    rounds = exchange_rounds(n)
    place = [order.index(o) for o in slots(rounds)]
    me = lax.axis_index("row").astype(jnp.int32).reshape(1)

    (own,) = call(
        begin,
        [jax.ShapeDtypeStruct((2, size, size), BF16)],
        (),
        (),
        [pltpu.SemaphoreType.DMA((2,))],
        0,
        "begin",
        (w1_blocks, w2_blocks),
    )
    fast = n <= 16
    panels = jax.ShapeDtypeStruct((nb, width, size), BF16)
    units = jax.ShapeDtypeStruct((FB, width, size), F32)
    pieces = [own]
    for masks in gather_rounds(n)[:-1]:
        moving = list(pieces)
        if fast and TIE and len(pieces) > 1:
            moving[0] = after(pieces[0], pieces[TIE])
        pieces = pieces + [swap(p, m, n) for m in masks for p in moving]
    moved = list(pieces)
    if fast:
        moved[PRE_SLOT], hidden, agrad, tok, tok_t, ct, ct_t, table = call(
            functools.partial(ready, nb, order),
            [jax.ShapeDtypeStruct(own.shape, BF16), units, units, panels, panels, panels, panels, jax.ShapeDtypeStruct((8, 128), jnp.int32)],
            (me, w1_rows, w1_cols, w2_rows, w2_cols),
            [tokens, cotangent, pieces[PRE_SLOT], *pieces[:EARLY]],
            name="ready",
            aliases=((2, 0),),
        )
    pieces = pieces + [swap(p, 1, n) for p in moved]
    late = list(range(EARLY, nb))
    if fast and TAIL:
        soon, late = late[:-TAIL], late[-TAIL:]
        hidden, agrad = call(
            functools.partial(more, soon),
            [units, units],
            (),
            [table, hidden, agrad, tok, ct, *[pieces[s] for s in soon]],
            [pltpu.VMEM((len(soon), width, size), F32)] * 2,
            name="more",
            aliases=((1, 0), (2, 1)),
        )
    weights = pieces if n <= 16 else [jnp.stack(pieces)]
    nw = len(weights)
    if n <= 16:
        lists = (me, w1_rows, w1_cols, w2_rows, w2_cols)

        def bind(kernel, *given):
            return lambda me, r1, c1, r2, c2, *refs: kernel(*given, me, order, r1, c1, r2, c2, *refs)
    else:
        assert place == list(range(nb))
        lists = (me, jnp.asarray(order, jnp.int32), w1_rows, w1_cols, w2_rows, w2_cols)

        def bind(kernel, *given):
            return functools.partial(kernel, *given)

    def blocks(count, dtype):
        return jax.ShapeDtypeStruct((count, 2, size, size), dtype)

    parts = len(rounds[0]) + 1
    half = nb // parts // 2
    work = 2 * nb * width * size * size
    outs = [panels, panels] + [blocks(half, BF16)] * parts + [blocks(half, F32)] * parts
    if fast:
        count = [half * len(g) for g in GROUPS]
        mine = GROUPS[:SPLIT] if SPLIT else GROUPS
        _, _, act, hgrad, *out = call(
            functools.partial(core, nb, parts, place, late, mine),
            [units, units, panels, panels] + [blocks(c, BF16) for c in count[:len(mine)]] + [blocks(c, F32) for c in count[:len(mine)]],
            (),
            [table, hidden, agrad, tok, tok_t, ct, ct_t, *[pieces[s] for s in late]],
            [pltpu.VMEM((len(late), width, size), F32)] * 2,
            4 * work,
            "middle",
            aliases=((1, 0), (2, 1)),
        )
    else:
        act, hgrad, *out = call(
            bind(middle, nb, nw, parts, place),
            outs,
            lists,
            [tokens, cotangent, *weights],
            [pltpu.VMEM((FB, width, size), F32), pltpu.VMEM((FB, width, size), F32)],
            4 * work,
            "middle",
        )
    model = jax.ShapeDtypeStruct((width, depth), BF16)
    total = pltpu.VMEM((depth // size, width, size), F32)
    if fast:
        stage = pltpu.VMEM((width, depth), BF16)
        output, input_grad = call(
            functools.partial(finish, nb),
            [model, model],
            (),
            [table, act, hgrad, *weights],
            [total, total, stage, stage, pltpu.SemaphoreType.DMA((2 * (depth // size // CHUNK),))],
            2 * work,
            "last",
            hbm_outs=True,
        )
    else:
        output, input_grad = call(bind(last, nb, nw), [model, model], lists, [act, hgrad, *weights], [total, total], 2 * work, "last")

    if fast:
        sends, keeps = out[:len(mine)], out[len(mine):]
        arrived = [swap(v, 1, n) for v in sends]
        if SPLIT:
            others = count[SPLIT:]
            made = call(
                functools.partial(rest, parts, place, GROUPS[SPLIT:]),
                [blocks(c, BF16) for c in others] + [blocks(c, F32) for c in others],
                (),
                [arrived[0], tok_t, ct_t, act, hgrad],
                name="rest",
            )
            keeps = [*keeps, *made[len(others):]]
            arrived = [*arrived, *[swap(v, 1, n) for v in made[:len(others)]]]

        def sums(held, arrived, shapes):
            return call(functools.partial(fold, len(shapes)), shapes, (), [held, *arrived], name="fold")

        landed = []
        for group, keep, near in zip(GROUPS, keeps, arrived):
            kept, leaving = sums(keep, [near], [blocks(len(group), F32), blocks(len(group), BF16)])
            beside = swap(leaving, 3, n)
            if group[-1] == 0:
                landed = [kept, beside, *landed]
            if group[0] != 0:
                (leaving,) = sums(kept, [beside], [blocks(1, BF16)])
                landed.append(swap(leaving, rounds[0][group[0] - 1], n))
    else:
        sends, keeps = out[:parts], out[parts:]
        near = rounds[1:][::-1]
        landed = []
        for i in range(parts):
            leaving, held = [sends[i]], keeps[i]
            for now, later in zip(near, [*near[1:], []]):
                arrived = [swap(v, m, n) for v, m in zip(leaving, now)]
                if later or i:
                    count = held.shape[0] // (len(later) + 1)
                    kept = blocks(count, F32 if later else BF16)
                    held, *leaving = call(
                        functools.partial(fold, len(later) + 1),
                        [kept] + [blocks(count, BF16)] * len(later),
                        (),
                        [held, *arrived],
                        name="fold",
                    )
            landed += [held, *arrived] if i == 0 else [swap(held, rounds[0][i - 1], n)]
    grad = jax.ShapeDtypeStruct((1, size, size), F32)
    first_grad, second_grad = call(
        functools.partial(close, (0.5 if fast else 1.0) / math.sqrt(width * n), 1 if fast else -1), [grad, grad], (), landed, name="close"
    )
    return (output, input_grad, first_grad, second_grad)


def solution(mesh):
    rows, blocks = P(("grp", "row"), None), P(("grp", "row"), None, None)
    return jax.shard_map(
        body,
        mesh=mesh,
        in_specs=(rows, rows, P("row", None, None), P(), P(), P("row", None, None), P(), P()),
        out_specs=(rows, rows, blocks, blocks),
        check_vma=False,
    )
```

```python
import functools
import math

import jax
import jax.numpy as jnp
from jax import lax
from jax.experimental import pallas as pl
from jax.experimental.pallas import tpu as pltpu
from jax.sharding import PartitionSpec as P

FB = 96
AHEAD = 10**10
CHUNK = 6
EARLY = 4
GROUPS = ((1,), (2,), (3,), (0,))
ROOT = math.sqrt(2.0 / math.pi)
CUBE = 0.044715
F32 = jnp.float32
BF16 = jnp.bfloat16
VMEM = pl.BlockSpec(memory_space=pltpu.VMEM)
ANY = pl.BlockSpec(memory_space=pl.ANY)
SMEM = pl.BlockSpec(memory_space=pltpu.SMEM)
ROUNDS = [[9, 5, 13], [3], [1]]


def bits(n):
    return [(1 << i) | 1 for i in range(n.bit_length() - 2, 0, -1)]


def gather_rounds(n):
    if n == 16:
        return ROUNDS
    return [[b] for b in bits(n)] + [[1]]


def exchange_rounds(n):
    if n == 16:
        return ROUNDS
    far, rounds = bits(n), []
    while far:
        a, far = far[0], far[1:]
        masks = [a]
        if far:
            b, far = far[0], far[1:]
            masks = [a, b, a ^ b]
        rounds.append(masks)
    return rounds + [[1]]


def slots(rounds):
    order = [0]
    for masks in rounds:
        order = order + [o ^ m for m in masks for o in order]
    return order


def swap(value, mask, n):
    return lax.ppermute(value, "row", [(i, i ^ mask) for i in range(n)])


def panel(ref, index, size):
    return ref[:, pl.ds(pl.multiple_of(index * size, size), size)]


def dot(a, b, dims):
    return lax.dot_general(a, b, (dims, ((), ())), preferred_element_type=F32)


def tanh_of(v, u):
    return jnp.tanh(v * (ROOT + ROOT * CUBE * u))


def gelu(v):
    h = 0.5 * v
    return h + h * tanh_of(v, v * v)


def gelu_slope(v):
    u = v * v
    t = tanh_of(v, u)
    g = 0.5 + 0.5 * t
    return g + (g * (1.0 - t)) * (v * (ROOT + 3.0 * ROOT * CUBE * u))


def twice_gelu(v):
    return v + v * tanh_of(v, v * v)


def twice_gelu_slope(v):
    u = v * v
    t = tanh_of(v, u)
    p = 1.0 + t
    return p + (p * (1.0 - t)) * (v * (ROOT + 3.0 * ROOT * CUBE * u))


def each(count, run):
    if count <= 16:
        for s in range(count):
            run(s)
    else:
        def step(s, _):
            run(s)
            return 0
        lax.fori_loop(0, count, step, 0)


class Lists:
    def __init__(self, me, order, r1, c1, r2, c2):
        self.block = lambda s: me[0] ^ order[s]
        self.r1 = lambda s: r1[self.block(s)]
        self.c1 = lambda s: c1[self.block(s)]
        self.r2 = lambda s: r2[self.block(s)]
        self.c2 = lambda s: c2[self.block(s)]


def begin(w1, w2, weights, sems):
    copies = [
        pltpu.make_async_copy(w1, weights.at[pl.ds(0, 1)], sems.at[0]),
        pltpu.make_async_copy(w2, weights.at[pl.ds(1, 1)], sems.at[1]),
    ]
    for copy in copies:
        copy.start()
    for copy in copies:
        copy.wait()


def middle(nb, nw, parts, place, me, order, r1, c1, r2, c2, tokens, cot, *refs):
    weights, (act, hgrad, *out), (hidden, agrad) = refs[:nw], refs[nw:-2], refs[-2:]
    sends, keeps = out[:parts], out[parts:]
    at = Lists(me, order, r1, c1, r2, c2)
    size = act.shape[-1]
    rest = nb // parts
    half = rest // 2

    def w(s, which):
        return weights[s][which] if nw > 1 else weights[0][s, which]

    def clear(s):
        zero = jnp.zeros(hidden.shape[1:], F32)
        for index in (at.c1(s), at.r2(s)):
            hidden[index] = zero
            agrad[index] = zero

    each(nb, clear)


    def first(s):
        hidden[at.c1(s)] += dot(panel(tokens, at.r1(s), size), w(s, 0), ((1,), (0,)))

    each(nb, first)

    def second(s):
        agrad[at.r2(s)] += dot(panel(cot, at.c2(s), size), w(s, 1), ((1,), (1,)))

    each(nb, second)

    def slope(s):
        c = at.c1(s)
        hgrad[s] = (agrad[c] * gelu_slope(hidden[c])).astype(BF16)

    def activate(s):
        act[s] = gelu(hidden[at.r2(s)]).astype(BF16)

    def put(i, q, which, value):
        def leave():
            sends[i][q - half, which] = value.astype(BF16)

        def stay():
            keeps[i][q, which] = value

        if isinstance(q, int):
            leave() if q >= half else stay()
        else:
            pl.when(q >= half)(leave)
            pl.when(q < half)(stay)

    def grads(i, q):
        s = i + parts * q
        s = place[s] if isinstance(q, int) else s
        activate(s)
        slope(s)
        put(i, q, 0, dot(panel(tokens, at.r1(s), size), hgrad[s], ((0,), (0,))))
        put(i, q, 1, dot(act[s], panel(cot, at.c2(s), size), ((0,), (0,))))

    for i in range(parts):
        each(rest, functools.partial(grads, i))


def finish(nb, table, act, hgrad, *refs):
    weights, (out, igrad, oacc, iacc, ostage, istage, sems) = refs[:nb], refs[nb:]
    size = act.shape[-1]
    count = oacc.shape[0]
    oacc[...] = jnp.zeros_like(oacc)
    iacc[...] = jnp.zeros_like(iacc)
    for s in range(nb):
        oacc[table[3, s]] += dot(act[s], weights[s][1], ((1,), (0,)))
        iacc[table[2, s]] += dot(hgrad[s], weights[s][0], ((1,), (1,)))
    copies = []
    for acc, stage, target in ((oacc, ostage, out), (iacc, istage, igrad)):
        for d in range(0, count, CHUNK):
            for e in range(d, d + CHUNK):
                stage[:, e * size:(e + 1) * size] = (0.5 * acc[e]).astype(BF16)
            at = (slice(None), pl.ds(d * size, CHUNK * size))
            copies.append(pltpu.make_async_copy(stage.at[at], target.at[at], sems.at[len(copies)]))
            copies[-1].start()
    for copy in copies:
        copy.wait()


def ready(nb, order, me, r1, c1, r2, c2, tokens, cot, piece, *refs):
    weights, (passed, hidden, agrad, tok, tok_t, ct, ct_t, table) = refs[:-8], refs[-8:]
    del piece, passed
    at = Lists(me, order, r1, c1, r2, c2)
    size = tok.shape[-1]
    zero = jnp.zeros(hidden.shape[1:], F32)
    for s in range(nb):
        hidden[at.c1(s)] = zero
        hidden[at.r2(s)] = zero
        agrad[at.c1(s)] = zero
        agrad[at.r2(s)] = zero
    lane = lax.broadcasted_iota(jnp.int32, table.shape, 1)
    row = lax.broadcasted_iota(jnp.int32, table.shape, 0)
    entries = jnp.zeros(table.shape, jnp.int32)
    for s in range(nb):
        value = jnp.where(row < 2, jnp.where(row == 0, at.c1(s), at.r2(s)), jnp.where(row == 2, at.r1(s), at.c2(s)))
        entries = jnp.where(lane == s, value, entries)
    table[...] = entries
    for s in range(nb):
        value = panel(tokens, at.r1(s), size)
        tok[s] = value
        tok_t[s] = value.T
        value = panel(cot, at.c2(s), size)
        ct[s] = value
        ct_t[s] = value.T
    for s, w in enumerate(weights):
        hidden[at.c1(s)] += dot(tok[s], w[0], ((1,), (0,)))
        agrad[at.r2(s)] += dot(ct[s], w[1], ((1,), (1,)))


def add_products(late, table, tok, ct, refs, hidden, agrad, prod, prod_t):
    for i, (s, w) in enumerate(zip(late, refs)):
        prod[i] = dot(tok[s], w[0], ((1,), (0,)))
        prod_t[i] = dot(ct[s], w[1], ((1,), (1,)))
    for i, s in enumerate(late):
        hidden[table[0, s]] += prod[i]
    for i, s in enumerate(late):
        agrad[table[1, s]] += prod_t[i]


def more(late, table, hidden_in, agrad_in, tok, ct, *refs):
    weights, (hidden, agrad, prod, prod_t) = refs[:-4], refs[-4:]
    del hidden_in, agrad_in
    add_products(late, table, tok, ct, weights, hidden, agrad, prod, prod_t)


def grads_of(groups, parts, place, tok_t, ct_t, act, hgrad, out):
    sends, keeps = out[:len(groups)], out[len(groups):]
    half = len(place) // parts // 2
    for group, send, keep in zip(groups, sends, keeps):
        for q in range(2 * half):
            for k, i in enumerate(group):
                s = place[i + parts * q]
                at = q % half * len(group) + k
                values = dot(tok_t[s], hgrad[s], ((1,), (0,))), dot(ct_t[s], act[s], ((1,), (0,)))
                for which, value in enumerate(values):
                    if q < half:
                        keep[at, which] = value
                    else:
                        send[at, which] = value.astype(BF16)


def core(nb, parts, place, late, groups, table, hidden_in, agrad_in, tok, tok_t, ct, ct_t, *refs):
    weights, (hidden, agrad, act, hgrad, *out, prod, prod_t) = refs[:len(late)], refs[len(late):]
    del hidden_in, agrad_in
    add_products(late, table, tok, ct, weights, hidden, agrad, prod, prod_t)
    for s in range(nb):
        act[s] = twice_gelu(hidden[table[1, s]]).astype(BF16)
        c = table[0, s]
        hgrad[s] = (agrad[c] * twice_gelu_slope(hidden[c])).astype(BF16)
    grads_of(groups, parts, place, tok_t, ct_t, act, hgrad, out)


def last(nb, nw, me, order, r1, c1, r2, c2, act, hgrad, *refs):
    weights, (out, igrad, oacc, iacc) = refs[:nw], refs[nw:]
    at = Lists(me, order, r1, c1, r2, c2)
    size = act.shape[-1]

    def w(s, which):
        return weights[s][which] if nw > 1 else weights[0][s, which]

    oacc[...] = jnp.zeros_like(oacc)
    iacc[...] = jnp.zeros_like(iacc)

    def one(s):
        oacc[at.c2(s)] += dot(act[s], w(s, 1), ((1,), (0,)))
        iacc[at.r1(s)] += dot(hgrad[s], w(s, 0), ((1,), (1,)))

    each(nb, one)
    for d in range(oacc.shape[0]):
        out[:, d * size:(d + 1) * size] = oacc[d].astype(BF16)
        igrad[:, d * size:(d + 1) * size] = iacc[d].astype(BF16)


def fold(parts, held, *refs):
    arrived, outs = refs[:-parts], refs[-parts:]
    count = outs[0].shape[0]
    for i, out in enumerate(outs):
        def one(q, i=i, out=out):
            value = held[count * i + q]
            for a in arrived:
                value = value + a[count * i + q].astype(F32)
            out[q] = value.astype(out.dtype)

        each(count, one)


def close(scale, turned, held, *refs):
    arrived, outs = refs[:-2], refs[-2:]
    for which, out in enumerate(outs):
        value = held[held.shape[0] - 1, which]
        for a in arrived:
            value = value + a[a.shape[0] - 1, which].astype(F32)
        value = value * scale
        out[0] = value.T if which == turned else value


def copy_after(value, other, out):
    del other
    out[...] = value[...]


def after(value, other):
    return call(copy_after, [jax.ShapeDtypeStruct(value.shape, value.dtype)], (), [value, other], (), AHEAD, "after")[0]


def call(kernel, outs, smem, args, scratch=(), flops=0, name=None, hbm_args=(), aliases=(), hbm_outs=False):
    size = sum(math.prod(a.shape) * a.dtype.itemsize for a in (*args, *outs))
    size += sum(math.prod(s.shape) * 4 for s in scratch)
    first = len(smem) + len(hbm_args)
    return pl.pallas_call(
        kernel,
        out_shape=outs,
        in_specs=[SMEM] * len(smem) + [ANY] * len(hbm_args) + [VMEM] * len(args),
        out_specs=[ANY if hbm_outs else VMEM] * len(outs),
        scratch_shapes=list(scratch),
        input_output_aliases={first + i: o for i, o in aliases},
        compiler_params=pltpu.CompilerParams(vmem_limit_bytes=min(size + (4 << 20), 60 << 20)),
        cost_estimate=pl.CostEstimate(flops=flops, bytes_accessed=size, transcendentals=0),
        name=name,
    )(*smem, *[pltpu.with_memory_space_constraint(a, pltpu.HBM) for a in hbm_args], *args)


def body(tokens, cotangent, w1_blocks, w1_rows, w1_cols, w2_blocks, w2_rows, w2_cols):
    n = lax.axis_size("row")
    nb = w1_rows.shape[0]
    width, depth = tokens.shape
    size = w1_blocks.shape[-1]
    order = slots(gather_rounds(n))
    rounds = exchange_rounds(n)
    place = [order.index(o) for o in slots(rounds)]
    me = lax.axis_index("row").astype(jnp.int32).reshape(1)

    (own,) = call(
        begin,
        [jax.ShapeDtypeStruct((2, size, size), BF16)],
        (),
        (),
        [pltpu.SemaphoreType.DMA((2,))],
        0,
        "begin",
        (w1_blocks, w2_blocks),
    )
    fast = n == 16
    panels = jax.ShapeDtypeStruct((nb, width, size), BF16)
    units = jax.ShapeDtypeStruct((FB, width, size), F32)
    pieces = [own]
    for masks in gather_rounds(n)[:-1]:
        moving = list(pieces)
        if fast and len(pieces) > 1:
            moving[0] = after(pieces[0], pieces[1])
        pieces = pieces + [swap(p, m, n) for m in masks for p in moving]
    moved = list(pieces)
    if fast:
        moved[3], hidden, agrad, tok, tok_t, ct, ct_t, table = call(
            functools.partial(ready, nb, order),
            [jax.ShapeDtypeStruct(own.shape, BF16), units, units, panels, panels, panels, panels, jax.ShapeDtypeStruct((8, 128), jnp.int32)],
            (me, w1_rows, w1_cols, w2_rows, w2_cols),
            [tokens, cotangent, pieces[3], *pieces[:EARLY]],
            name="ready",
            aliases=((2, 0),),
        )
    pieces = pieces + [swap(p, 1, n) for p in moved]
    if fast:
        soon, late = list(range(EARLY, nb - 1)), [nb - 1]
        hidden, agrad = call(
            functools.partial(more, soon),
            [units, units],
            (),
            [table, hidden, agrad, tok, ct, *[pieces[s] for s in soon]],
            [pltpu.VMEM((len(soon), width, size), F32)] * 2,
            name="more",
            aliases=((1, 0), (2, 1)),
        )
    weights = pieces if fast else [jnp.stack(pieces)]
    nw = len(weights)
    if fast:
        lists = (me, w1_rows, w1_cols, w2_rows, w2_cols)

        def bind(kernel, *given):
            return lambda me, r1, c1, r2, c2, *refs: kernel(*given, me, order, r1, c1, r2, c2, *refs)
    else:
        assert place == list(range(nb))
        lists = (me, jnp.asarray(order, jnp.int32), w1_rows, w1_cols, w2_rows, w2_cols)

        def bind(kernel, *given):
            return functools.partial(kernel, *given)

    def blocks(count, dtype):
        return jax.ShapeDtypeStruct((count, 2, size, size), dtype)

    parts = len(rounds[0]) + 1
    half = nb // parts // 2
    work = 2 * nb * width * size * size
    outs = [panels, panels] + [blocks(half, BF16)] * parts + [blocks(half, F32)] * parts
    if fast:
        count = [half * len(g) for g in GROUPS]
        _, _, act, hgrad, *out = call(
            functools.partial(core, nb, parts, place, late, GROUPS),
            [units, units, panels, panels] + [blocks(c, BF16) for c in count] + [blocks(c, F32) for c in count],
            (),
            [table, hidden, agrad, tok, tok_t, ct, ct_t, *[pieces[s] for s in late]],
            [pltpu.VMEM((len(late), width, size), F32)] * 2,
            4 * work,
            "middle",
            aliases=((1, 0), (2, 1)),
        )
    else:
        act, hgrad, *out = call(
            bind(middle, nb, nw, parts, place),
            outs,
            lists,
            [tokens, cotangent, *weights],
            [pltpu.VMEM((FB, width, size), F32), pltpu.VMEM((FB, width, size), F32)],
            4 * work,
            "middle",
        )
    model = jax.ShapeDtypeStruct((width, depth), BF16)
    total = pltpu.VMEM((depth // size, width, size), F32)
    if fast:
        stage = pltpu.VMEM((width, depth), BF16)
        output, input_grad = call(
            functools.partial(finish, nb),
            [model, model],
            (),
            [table, act, hgrad, *weights],
            [total, total, stage, stage, pltpu.SemaphoreType.DMA((2 * (depth // size // CHUNK),))],
            2 * work,
            "last",
            hbm_outs=True,
        )
    else:
        output, input_grad = call(bind(last, nb, nw), [model, model], lists, [act, hgrad, *weights], [total, total], 2 * work, "last")

    if fast:
        sends, keeps = out[:len(GROUPS)], out[len(GROUPS):]
        arrived = [swap(v, 1, n) for v in sends]

        def sums(held, arrived, shapes):
            return call(functools.partial(fold, len(shapes)), shapes, (), [held, *arrived], name="fold")

        landed = []
        for group, keep, near in zip(GROUPS, keeps, arrived):
            kept, leaving = sums(keep, [near], [blocks(len(group), F32), blocks(len(group), BF16)])
            beside = swap(leaving, 3, n)
            if group[-1] == 0:
                landed = [kept, beside, *landed]
            if group[0] != 0:
                (leaving,) = sums(kept, [beside], [blocks(1, BF16)])
                landed.append(swap(leaving, rounds[0][group[0] - 1], n))
    else:
        sends, keeps = out[:parts], out[parts:]
        near = rounds[1:][::-1]
        landed = []
        for i in range(parts):
            leaving, held = [sends[i]], keeps[i]
            for now, later in zip(near, [*near[1:], []]):
                arrived = [swap(v, m, n) for v, m in zip(leaving, now)]
                if later or i:
                    count = held.shape[0] // (len(later) + 1)
                    kept = blocks(count, F32 if later else BF16)
                    held, *leaving = call(
                        functools.partial(fold, len(later) + 1),
                        [kept] + [blocks(count, BF16)] * len(later),
                        (),
                        [held, *arrived],
                        name="fold",
                    )
            landed += [held, *arrived] if i == 0 else [swap(held, rounds[0][i - 1], n)]
    grad = jax.ShapeDtypeStruct((1, size, size), F32)
    first_grad, second_grad = call(
        functools.partial(close, (0.5 if fast else 1.0) / math.sqrt(width * n), 1 if fast else -1), [grad, grad], (), landed, name="close"
    )
    return (output, input_grad, first_grad, second_grad)


def solution(mesh):
    rows, blocks = P(("grp", "row"), None), P(("grp", "row"), None, None)
    return jax.shard_map(
        body,
        mesh=mesh,
        in_specs=(rows, rows, P("row", None, None), P(), P(), P("row", None, None), P(), P()),
        out_specs=(rows, rows, blocks, blocks),
        check_vma=False,
    )
```

```python
import functools
import math

import jax
import jax.numpy as jnp
from jax import lax
from jax.experimental import pallas as pl
from jax.experimental.pallas import tpu as pltpu
from jax.sharding import PartitionSpec as P

FB = 96
AHEAD = 10**10
CHUNK = 6
EARLY = 4
GROUPS = ((1,), (2,), (0,), (3,))
ROOT = math.sqrt(2.0 / math.pi)
CUBE = 0.044715
F32 = jnp.float32
BF16 = jnp.bfloat16
VMEM = pl.BlockSpec(memory_space=pltpu.VMEM)
ANY = pl.BlockSpec(memory_space=pl.ANY)
SMEM = pl.BlockSpec(memory_space=pltpu.SMEM)
ROUNDS = [[9, 5, 13], [3], [1]]


def bits(n):
    return [(1 << i) | 1 for i in range(n.bit_length() - 2, 0, -1)]


def gather_rounds(n):
    if n == 16:
        return ROUNDS
    return [[b] for b in bits(n)] + [[1]]


def exchange_rounds(n):
    if n == 16:
        return ROUNDS
    far, rounds = bits(n), []
    while far:
        a, far = far[0], far[1:]
        masks = [a]
        if far:
            b, far = far[0], far[1:]
            masks = [a, b, a ^ b]
        rounds.append(masks)
    return rounds + [[1]]


def slots(rounds):
    order = [0]
    for masks in rounds:
        order = order + [o ^ m for m in masks for o in order]
    return order


def swap(value, mask, n):
    return lax.ppermute(value, "row", [(i, i ^ mask) for i in range(n)])


def panel(ref, index, size):
    return ref[:, pl.ds(pl.multiple_of(index * size, size), size)]


def dot(a, b, dims):
    return lax.dot_general(a, b, (dims, ((), ())), preferred_element_type=F32)


def tanh_of(v, u):
    return jnp.tanh(v * (ROOT + ROOT * CUBE * u))


def gelu(v):
    h = 0.5 * v
    return h + h * tanh_of(v, v * v)


def gelu_slope(v):
    u = v * v
    t = tanh_of(v, u)
    g = 0.5 + 0.5 * t
    return g + (g * (1.0 - t)) * (v * (ROOT + 3.0 * ROOT * CUBE * u))


def twice_gelu(v):
    return v + v * tanh_of(v, v * v)


def twice_gelu_slope(v):
    u = v * v
    t = tanh_of(v, u)
    p = 1.0 + t
    return p + (p * (1.0 - t)) * (v * (ROOT + 3.0 * ROOT * CUBE * u))


def each(count, run):
    if count <= 16:
        for s in range(count):
            run(s)
    else:
        def step(s, _):
            run(s)
            return 0
        lax.fori_loop(0, count, step, 0)


class Lists:
    def __init__(self, me, order, r1, c1, r2, c2):
        self.block = lambda s: me[0] ^ order[s]
        self.r1 = lambda s: r1[self.block(s)]
        self.c1 = lambda s: c1[self.block(s)]
        self.r2 = lambda s: r2[self.block(s)]
        self.c2 = lambda s: c2[self.block(s)]


def begin(w1, w2, weights, sems):
    copies = [
        pltpu.make_async_copy(w1, weights.at[pl.ds(0, 1)], sems.at[0]),
        pltpu.make_async_copy(w2, weights.at[pl.ds(1, 1)], sems.at[1]),
    ]
    for copy in copies:
        copy.start()
    for copy in copies:
        copy.wait()


def middle(nb, nw, parts, place, me, order, r1, c1, r2, c2, tokens, cot, *refs):
    weights, (act, hgrad, *out), (hidden, agrad) = refs[:nw], refs[nw:-2], refs[-2:]
    sends, keeps = out[:parts], out[parts:]
    at = Lists(me, order, r1, c1, r2, c2)
    size = act.shape[-1]
    rest = nb // parts
    half = rest // 2

    def w(s, which):
        return weights[s][which] if nw > 1 else weights[0][s, which]

    def clear(s):
        zero = jnp.zeros(hidden.shape[1:], F32)
        for index in (at.c1(s), at.r2(s)):
            hidden[index] = zero
            agrad[index] = zero

    each(nb, clear)


    def first(s):
        hidden[at.c1(s)] += dot(panel(tokens, at.r1(s), size), w(s, 0), ((1,), (0,)))

    each(nb, first)

    def second(s):
        agrad[at.r2(s)] += dot(panel(cot, at.c2(s), size), w(s, 1), ((1,), (1,)))

    each(nb, second)

    def slope(s):
        c = at.c1(s)
        hgrad[s] = (agrad[c] * gelu_slope(hidden[c])).astype(BF16)

    def activate(s):
        act[s] = gelu(hidden[at.r2(s)]).astype(BF16)

    def put(i, q, which, value):
        def leave():
            sends[i][q - half, which] = value.astype(BF16)

        def stay():
            keeps[i][q, which] = value

        if isinstance(q, int):
            leave() if q >= half else stay()
        else:
            pl.when(q >= half)(leave)
            pl.when(q < half)(stay)

    def grads(i, q):
        s = i + parts * q
        s = place[s] if isinstance(q, int) else s
        activate(s)
        slope(s)
        put(i, q, 0, dot(panel(tokens, at.r1(s), size), hgrad[s], ((0,), (0,))))
        put(i, q, 1, dot(act[s], panel(cot, at.c2(s), size), ((0,), (0,))))

    for i in range(parts):
        each(rest, functools.partial(grads, i))


def finish(nb, table, act, hgrad, *refs):
    weights, (out, igrad, oacc, iacc, ostage, istage, sems) = refs[:nb], refs[nb:]
    size = act.shape[-1]
    count = oacc.shape[0]
    oacc[...] = jnp.zeros_like(oacc)
    iacc[...] = jnp.zeros_like(iacc)
    for s in range(nb):
        oacc[table[3, s]] += dot(act[s], weights[s][1], ((1,), (0,)))
        iacc[table[2, s]] += dot(hgrad[s], weights[s][0], ((1,), (1,)))
    copies = []
    for acc, stage, target in ((oacc, ostage, out), (iacc, istage, igrad)):
        for d in range(0, count, CHUNK):
            for e in range(d, d + CHUNK):
                stage[:, e * size:(e + 1) * size] = (0.5 * acc[e]).astype(BF16)
            at = (slice(None), pl.ds(d * size, CHUNK * size))
            copies.append(pltpu.make_async_copy(stage.at[at], target.at[at], sems.at[len(copies)]))
            copies[-1].start()
    for copy in copies:
        copy.wait()


def ready(nb, order, r1, c1, r2, c2, tokens, cot, piece, *refs):
    weights, (passed, hidden, agrad, tok, tok_t, ct, ct_t, table, lists) = refs[:-9], refs[-9:]
    del piece, passed
    me = lax.axis_index("row")
    for k, ref in enumerate((c1, r2, r1, c2)):
        lists[k:k + 1, :nb] = ref[...]
    lane = lax.broadcasted_iota(jnp.int32, lists.shape, 1)
    value, bit = lists[...], 1
    while bit < nb:
        other = jnp.where(lane & bit == 0, pltpu.roll(value, 128 - bit, 1), pltpu.roll(value, bit, 1))
        value = jnp.where(me & bit == 0, value, other)
        bit *= 2
    lists[...] = value
    c1, r2, r1, c2 = ([lists[k, o] for o in order] for k in range(4))
    size = tok.shape[-1]
    zero = jnp.zeros(hidden.shape[1:], F32)
    for s in range(nb):
        hidden[c1[s]] = zero
        hidden[r2[s]] = zero
        agrad[c1[s]] = zero
        agrad[r2[s]] = zero
    lane = lax.broadcasted_iota(jnp.int32, table.shape, 1)
    row = lax.broadcasted_iota(jnp.int32, table.shape, 0)
    entries = jnp.zeros(table.shape, jnp.int32)
    for s in range(nb):
        value = jnp.where(row < 2, jnp.where(row == 0, c1[s], r2[s]), jnp.where(row == 2, r1[s], c2[s]))
        entries = jnp.where(lane == s, value, entries)
    table[...] = entries
    for s in range(nb):
        value = panel(tokens, r1[s], size)
        tok[s] = value
        tok_t[s] = value.T
        value = panel(cot, c2[s], size)
        ct[s] = value
        ct_t[s] = value.T
    for s, w in enumerate(weights):
        hidden[c1[s]] += dot(tok[s], w[0], ((1,), (0,)))
        agrad[r2[s]] += dot(ct[s], w[1], ((1,), (1,)))


def add_products(late, table, tok, ct, refs, hidden, agrad, prod, prod_t):
    for i, (s, w) in enumerate(zip(late, refs)):
        prod[i] = dot(tok[s], w[0], ((1,), (0,)))
        prod_t[i] = dot(ct[s], w[1], ((1,), (1,)))
    for i, s in enumerate(late):
        hidden[table[0, s]] += prod[i]
    for i, s in enumerate(late):
        agrad[table[1, s]] += prod_t[i]


def more(late, table, hidden_in, agrad_in, tok, ct, *refs):
    weights, (hidden, agrad, prod, prod_t) = refs[:-4], refs[-4:]
    del hidden_in, agrad_in
    add_products(late, table, tok, ct, weights, hidden, agrad, prod, prod_t)


def grads_of(groups, parts, place, tok_t, ct_t, act, hgrad, out):
    sends, keeps = out[:len(groups)], out[len(groups):]
    half = len(place) // parts // 2
    for group, send, keep in zip(groups, sends, keeps):
        for q in range(2 * half):
            for k, i in enumerate(group):
                s = place[i + parts * q]
                at = q % half * len(group) + k
                values = dot(tok_t[s], hgrad[s], ((1,), (0,))), dot(ct_t[s], act[s], ((1,), (0,)))
                for which, value in enumerate(values):
                    if q < half:
                        keep[at, which] = value
                    else:
                        send[at, which] = value.astype(BF16)


def core(nb, parts, place, late, groups, table, hidden_in, agrad_in, tok, tok_t, ct, ct_t, *refs):
    weights, (hidden, agrad, act, hgrad, *out, prod, prod_t) = refs[:len(late)], refs[len(late):]
    del hidden_in, agrad_in
    add_products(late, table, tok, ct, weights, hidden, agrad, prod, prod_t)
    for s in range(nb):
        act[s] = twice_gelu(hidden[table[1, s]]).astype(BF16)
        c = table[0, s]
        hgrad[s] = (agrad[c] * twice_gelu_slope(hidden[c])).astype(BF16)
    grads_of(groups, parts, place, tok_t, ct_t, act, hgrad, out)


def last(nb, nw, me, order, r1, c1, r2, c2, act, hgrad, *refs):
    weights, (out, igrad, oacc, iacc) = refs[:nw], refs[nw:]
    at = Lists(me, order, r1, c1, r2, c2)
    size = act.shape[-1]

    def w(s, which):
        return weights[s][which] if nw > 1 else weights[0][s, which]

    oacc[...] = jnp.zeros_like(oacc)
    iacc[...] = jnp.zeros_like(iacc)

    def one(s):
        oacc[at.c2(s)] += dot(act[s], w(s, 1), ((1,), (0,)))
        iacc[at.r1(s)] += dot(hgrad[s], w(s, 0), ((1,), (1,)))

    each(nb, one)
    for d in range(oacc.shape[0]):
        out[:, d * size:(d + 1) * size] = oacc[d].astype(BF16)
        igrad[:, d * size:(d + 1) * size] = iacc[d].astype(BF16)


def fold(parts, held, *refs):
    arrived, outs = refs[:-parts], refs[-parts:]
    count = outs[0].shape[0]
    for i, out in enumerate(outs):
        def one(q, i=i, out=out):
            value = held[count * i + q]
            for a in arrived:
                value = value + a[count * i + q].astype(F32)
            out[q] = value.astype(out.dtype)

        each(count, one)


def close(scale, turned, held, *refs):
    arrived, outs = refs[:-2], refs[-2:]
    for which, out in enumerate(outs):
        value = held[held.shape[0] - 1, which]
        for a in arrived:
            value = value + a[a.shape[0] - 1, which].astype(F32)
        value = value * scale
        out[0] = value.T if which == turned else value


def copy_after(value, other, out):
    del other
    out[...] = value[...]


def after(value, other):
    return call(copy_after, [jax.ShapeDtypeStruct(value.shape, value.dtype)], (), [value, other], (), AHEAD, "after")[0]


def call(kernel, outs, smem, args, scratch=(), flops=0, name=None, hbm_args=(), aliases=(), hbm_outs=False):
    size = sum(math.prod(a.shape) * a.dtype.itemsize for a in (*args, *outs))
    size += sum(math.prod(s.shape) * 4 for s in scratch)
    first = len(smem) + len(hbm_args)
    return pl.pallas_call(
        kernel,
        out_shape=outs,
        in_specs=[SMEM] * len(smem) + [ANY] * len(hbm_args) + [VMEM] * len(args),
        out_specs=[ANY if hbm_outs else VMEM] * len(outs),
        scratch_shapes=list(scratch),
        input_output_aliases={first + i: o for i, o in aliases},
        compiler_params=pltpu.CompilerParams(vmem_limit_bytes=min(size + (4 << 20), 60 << 20)),
        cost_estimate=pl.CostEstimate(flops=flops, bytes_accessed=size, transcendentals=0),
        name=name,
    )(*smem, *[pltpu.with_memory_space_constraint(a, pltpu.HBM) for a in hbm_args], *args)


def body(tokens, cotangent, w1_blocks, w1_rows, w1_cols, w2_blocks, w2_rows, w2_cols):
    n = lax.axis_size("row")
    nb = w1_rows.shape[0]
    width, depth = tokens.shape
    size = w1_blocks.shape[-1]
    order = slots(gather_rounds(n))
    rounds = exchange_rounds(n)
    place = [order.index(o) for o in slots(rounds)]
    me = lax.axis_index("row").astype(jnp.int32).reshape(1)

    (own,) = call(
        begin,
        [jax.ShapeDtypeStruct((2, size, size), BF16)],
        (),
        (),
        [pltpu.SemaphoreType.DMA((2,))],
        0,
        "begin",
        (w1_blocks, w2_blocks),
    )
    fast = n == 16
    panels = jax.ShapeDtypeStruct((nb, width, size), BF16)
    units = jax.ShapeDtypeStruct((FB, width, size), F32)
    pieces = [own]
    for masks in gather_rounds(n)[:-1]:
        moving = list(pieces)
        if fast and len(pieces) > 1:
            moving[0] = after(pieces[0], pieces[1])
        pieces = pieces + [swap(p, m, n) for m in masks for p in moving]
    moved = list(pieces)
    if fast:
        moved[3], hidden, agrad, tok, tok_t, ct, ct_t, table = call(
            functools.partial(ready, nb, order),
            [jax.ShapeDtypeStruct(own.shape, BF16), units, units, panels, panels, panels, panels, jax.ShapeDtypeStruct((8, 128), jnp.int32)],
            (),
            [*[v.reshape(1, nb) for v in (w1_rows, w1_cols, w2_rows, w2_cols)], tokens, cotangent, pieces[3], *pieces[:EARLY]],
            [pltpu.VMEM((8, 128), jnp.int32)],
            name="ready",
            aliases=((6, 0),),
        )
    pieces = pieces + [swap(p, 1, n) for p in moved]
    if fast:
        soon, late = list(range(EARLY, nb - 1)), [nb - 1]
        hidden, agrad = call(
            functools.partial(more, soon),
            [units, units],
            (),
            [table, hidden, agrad, tok, ct, *[pieces[s] for s in soon]],
            [pltpu.VMEM((len(soon), width, size), F32)] * 2,
            name="more",
            aliases=((1, 0), (2, 1)),
        )
    weights = pieces if fast else [jnp.stack(pieces)]
    nw = len(weights)
    if fast:
        lists = (me, w1_rows, w1_cols, w2_rows, w2_cols)

        def bind(kernel, *given):
            return lambda me, r1, c1, r2, c2, *refs: kernel(*given, me, order, r1, c1, r2, c2, *refs)
    else:
        assert place == list(range(nb))
        lists = (me, jnp.asarray(order, jnp.int32), w1_rows, w1_cols, w2_rows, w2_cols)

        def bind(kernel, *given):
            return functools.partial(kernel, *given)

    def blocks(count, dtype):
        return jax.ShapeDtypeStruct((count, 2, size, size), dtype)

    parts = len(rounds[0]) + 1
    half = nb // parts // 2
    work = 2 * nb * width * size * size
    outs = [panels, panels] + [blocks(half, BF16)] * parts + [blocks(half, F32)] * parts
    if fast:
        count = [half * len(g) for g in GROUPS]
        _, _, act, hgrad, *out = call(
            functools.partial(core, nb, parts, place, late, GROUPS),
            [units, units, panels, panels] + [blocks(c, BF16) for c in count] + [blocks(c, F32) for c in count],
            (),
            [table, hidden, agrad, tok, tok_t, ct, ct_t, *[pieces[s] for s in late]],
            [pltpu.VMEM((len(late), width, size), F32)] * 2,
            4 * work,
            "middle",
            aliases=((1, 0), (2, 1)),
        )
    else:
        act, hgrad, *out = call(
            bind(middle, nb, nw, parts, place),
            outs,
            lists,
            [tokens, cotangent, *weights],
            [pltpu.VMEM((FB, width, size), F32), pltpu.VMEM((FB, width, size), F32)],
            4 * work,
            "middle",
        )
    model = jax.ShapeDtypeStruct((width, depth), BF16)
    total = pltpu.VMEM((depth // size, width, size), F32)
    if fast:
        stage = pltpu.VMEM((width, depth), BF16)
        output, input_grad = call(
            functools.partial(finish, nb),
            [model, model],
            (),
            [table, act, hgrad, *weights],
            [total, total, stage, stage, pltpu.SemaphoreType.DMA((2 * (depth // size // CHUNK),))],
            2 * work,
            "last",
            hbm_outs=True,
        )
    else:
        output, input_grad = call(bind(last, nb, nw), [model, model], lists, [act, hgrad, *weights], [total, total], 2 * work, "last")

    if fast:
        sends, keeps = out[:len(GROUPS)], out[len(GROUPS):]
        arrived = [swap(v, 1, n) for v in sends]

        def sums(held, arrived, shapes):
            return call(functools.partial(fold, len(shapes)), shapes, (), [held, *arrived], name="fold")

        landed = []
        for group, keep, near in zip(GROUPS, keeps, arrived):
            kept, leaving = sums(keep, [near], [blocks(len(group), F32), blocks(len(group), BF16)])
            beside = swap(leaving, 3, n)
            if group[-1] == 0:
                landed = [kept, beside, *landed]
            if group[0] != 0:
                (leaving,) = sums(kept, [beside], [blocks(1, BF16)])
                landed.append(swap(leaving, rounds[0][group[0] - 1], n))
    else:
        sends, keeps = out[:parts], out[parts:]
        near = rounds[1:][::-1]
        landed = []
        for i in range(parts):
            leaving, held = [sends[i]], keeps[i]
            for now, later in zip(near, [*near[1:], []]):
                arrived = [swap(v, m, n) for v, m in zip(leaving, now)]
                if later or i:
                    count = held.shape[0] // (len(later) + 1)
                    kept = blocks(count, F32 if later else BF16)
                    held, *leaving = call(
                        functools.partial(fold, len(later) + 1),
                        [kept] + [blocks(count, BF16)] * len(later),
                        (),
                        [held, *arrived],
                        name="fold",
                    )
            landed += [held, *arrived] if i == 0 else [swap(held, rounds[0][i - 1], n)]
    grad = jax.ShapeDtypeStruct((1, size, size), F32)
    first_grad, second_grad = call(
        functools.partial(close, (0.5 if fast else 1.0) / math.sqrt(width * n), 1 if fast else -1), [grad, grad], (), landed, name="close"
    )
    return (output, input_grad, first_grad, second_grad)


def solution(mesh):
    rows, blocks = P(("grp", "row"), None), P(("grp", "row"), None, None)
    return jax.shard_map(
        body,
        mesh=mesh,
        in_specs=(rows, rows, P("row", None, None), P(), P(), P("row", None, None), P(), P()),
        out_specs=(rows, rows, blocks, blocks),
        check_vma=False,
    )
```
